128 devices in a mesh: seq: 32 (over z_lo, y, x), dp: 4 (over z_hi, core).
Axes of the slice: x: 4, y: 4, z: 4 (z_hi: 2, z_lo: 2; z = z_hi * 2 + z_lo), core: 2. Of those that a mesh axis runs over, the one named last changes fastest.
Arguments:
- inputs: bfloat16 [4, 16384, 1024], P('dp', 'seq'), may hold values from -600 to 600
- cotangent: bfloat16 [4, 16384, 1024], P('dp', 'seq'), may hold values from -6 to 6
- gain: float32 [1024], replicated, may hold values from 0.5 to 1.5
- w_qkv: bfloat16 [1024, 3072], replicated, may hold values from -1.25 to 1.25
- w_out: bfloat16 [1024, 1024], replicated, may hold values from -0.1875 to 0.1875
- segment_ids: int32 [4, 16384], P('dp'), may hold values from 0 to 15, never falling along the last dimension, each value on 1 to 2048 neighbouring positions
Outputs:
- grad_inputs: bfloat16 [4, 16384, 1024], P('dp', 'seq')
- grad_qkv_weight: float32 [1024, 3072], P('seq')
The draws below stay inside these ranges and needn't reach their ends.
Inputs may be any that keep to these rules, and one draw needn't show every extreme that they name: `segment_ids`: each row is non-decreasing; every document is 1 to 2048 bytes long and one is exactly 2048.
All inputs are finite; a program needn't handle non-finite values.
Results may differ from the reference program's by a relative error of at most 0.03.
Values may be sent and summed in bfloat16 or wider, within the bound.
A program may use at most 192 MiB of HBM per device.

```python
import math
import jax
import jax.numpy as jnp
import numpy as np
from jax import lax

D = 1024
HEADS = 16
WINDOW = 512
TOK_DEV = 512
SEQLEN = 16384
DOCS = 16
DOC_MOST = 2048
N_DP = 4


def draw_inputs(key, part):
    first, second, third = jax.random.split(jax.random.fold_in(key, 11), 3)
    base = jnp.clip(jax.random.normal(first, (N_DP, SEQLEN, D), jnp.float32), -4.0, 4.0)
    row_scale = jnp.exp(jax.random.uniform(second, (N_DP, SEQLEN, 1), jnp.float32, 0.0, math.log(10.0)))
    col_scale = jnp.exp(jax.random.uniform(third, (D,), jnp.float32, 0.0, math.log(10.0)))
    return (base * row_scale * col_scale).astype(jnp.bfloat16)


def draw_w_qkv(key, part):
    first = jax.random.fold_in(jax.random.fold_in(key, 23), 0)
    base = jnp.clip(jax.random.normal(first, (D, 3 * D), jnp.float32), -5.0, 5.0) * D ** (-0.5)
    return base.astype(jnp.bfloat16)


def steps_of(rng, extent, cuts, least, top_value):
    def one(axis_at, blocks):
        draws = jax.random.uniform(jax.random.fold_in(jax.random.fold_in(rng, 6), axis_at), (blocks,), jnp.float32, least / len(cuts), top_value / len(cuts))
        return jnp.repeat(jnp.exp(draws), extent[axis_at] // blocks).reshape((-1,) + (1,) * (len(extent) - axis_at - 1))

    level = one(*cuts[0])
    for cut in cuts[1:]:
        level = level * one(*cut)
    return level


def length_profile(count, total, reach, lean):
    portions = [(1 << 20) // math.isqrt(standing ** lean) + 1 for standing in range(2, count + 1)]
    rest, holding = total - reach - (count - 1), [1] * (count - 1)
    while rest > 0:
        free = [i for i in range(count - 1) if holding[i] < reach]
        pool, left = sum([portions[i] for i in free]), rest
        for i in free:
            extra = min(reach - holding[i], max(1, left * portions[i] // pool), rest)
            holding[i] = holding[i] + extra
            rest = rest - extra
    return np.array([reach] + holding)


def uneven_parts(key, amount, total, bound, slope):
    if amount == 2:
        one = jax.random.randint(key, (), max(1, total - bound), min(bound, total - 1) + 1)
        return jnp.stack([one, total - one])
    tallies = jnp.asarray(length_profile(amount, total, bound, slope), jnp.int32)
    couples = (amount - 1) // 2
    source_of, sink = tallies[1:1 + 2 * couples:2], tallies[2:2 + 2 * couples:2]
    room = jnp.minimum(source_of - 1, bound - sink)
    moved = jax.random.randint(jax.random.fold_in(key, 1), (couples,), 0, 1 << 20) % (room + 1)
    tallies = tallies.at[1:1 + 2 * couples:2].set(source_of - moved).at[2:2 + 2 * couples:2].set(sink + moved)
    return tallies[jax.random.permutation(jax.random.fold_in(key, 2), amount)]


def noise(rng, extent, spread, most, cuts=(), held_as=jnp.bfloat16):
    factor_of = steps_of(rng, extent, cuts, -0.22, 0.18) if cuts else 1.0
    entries = jax.random.normal(rng, extent, jnp.float32) * spread * factor_of
    return jnp.minimum(jnp.maximum(entries, -most), most).astype(held_as)


def setup_inputs(seed: int = 0) -> dict:
    seeds = jax.random.split(jax.random.key(seed), 7)
    inputs = draw_inputs(jax.random.fold_in(seeds[6], 71), 0)
    cotangent = noise(seeds[1], (N_DP, SEQLEN, D), 1.0, 6.0, ((0, 4), (1, 32)))
    gain = jnp.clip(1.0 + 0.1 * jax.random.normal(seeds[2], (D,), jnp.float32), 0.5, 1.5)
    w_qkv = draw_w_qkv(jax.random.fold_in(seeds[6], 71), 0)
    w_out = noise(seeds[4], (D, D), D ** -0.5, 0.1875)
    segment_ids = jax.vmap(lambda own: jnp.searchsorted(jnp.cumsum(uneven_parts(own, DOCS, SEQLEN, DOC_MOST, 2)), jnp.arange(SEQLEN), side="right"))(jax.random.split(seeds[5], N_DP)).reshape((N_DP, SEQLEN)).astype(jnp.int32)
    return {"inputs": inputs, "cotangent": cotangent, "gain": gain, "w_qkv": w_qkv, "w_out": w_out, "segment_ids": segment_ids}


EPS = 1e-05

def soft_probs(qblk, kblk, pos_q, pos_k, seg_q, seg_k):
    qh = qblk.reshape(qblk.shape[0], HEADS, -1).astype(jnp.float32)
    kh = kblk.reshape(kblk.shape[0], HEADS, -1).astype(jnp.float32)
    scores = jnp.einsum('qhd,khd->hqk', qh, kh) * qh.shape[2] ** (-0.5)
    allowed = (pos_k[None, :] <= pos_q[:, None]) & (pos_q[:, None] - pos_k[None, :] < WINDOW) & (seg_k[None, :] == seg_q[:, None])
    scores = jnp.where(allowed[None], scores, -1e+30)
    top = lax.optimization_barrier(jnp.max(scores, axis=2, keepdims=True))
    expo = jnp.exp(scores - top)
    return expo / lax.optimization_barrier(jnp.sum(expo, axis=2, keepdims=True))

def lowered(value):
    return lax.optimization_barrier(value.astype(jnp.bfloat16)).astype(jnp.float32)

def one_sequence(x, grad_out, gain, w_qkv, w_out, seg):
    length = x.shape[0]
    width = x.shape[1]
    xf = x.astype(jnp.float32)
    inv_rms = lax.rsqrt(lax.optimization_barrier(jnp.mean(xf * xf, axis=1, keepdims=True)) + EPS)
    normal_x = xf * inv_rms
    normed = (normal_x * gain).astype(jnp.bfloat16)
    qkv = jnp.dot(normed, w_qkv, preferred_element_type=jnp.float32).astype(jnp.bfloat16)
    queries = qkv[:, :width]
    keys_pad = jnp.concatenate([jnp.zeros((WINDOW, width), jnp.bfloat16), qkv[:, width:2 * width]], 0)
    values_pad = jnp.concatenate([jnp.zeros((WINDOW, width), jnp.bfloat16), qkv[:, 2 * width:]], 0)
    seg_pad = jnp.concatenate([jnp.full((WINDOW,), -1, jnp.int32), seg.astype(jnp.int32)], 0)
    block = min(512, TOK_DEV)
    count = length // block
    span = WINDOW + block
    scale = (width // HEADS) ** (-0.5)

    def pieces(first):
        pos_q = (first + jnp.arange(block)).astype(jnp.int32)
        pos_k = (first - WINDOW + jnp.arange(span)).astype(jnp.int32)
        qblk = lax.dynamic_slice_in_dim(queries, first, block, 0)
        kblk = lax.dynamic_slice_in_dim(keys_pad, first, span, 0)
        vblk = lax.dynamic_slice_in_dim(values_pad, first, span, 0)
        seg_q = lax.dynamic_slice_in_dim(seg_pad, first + WINDOW, block, 0)
        seg_k = lax.dynamic_slice_in_dim(seg_pad, first, span, 0)
        probs = soft_probs(qblk, kblk, pos_q, pos_k, seg_q, seg_k)
        return (qblk, kblk, vblk, probs)

    def forward_block(index):
        first = (index * block).astype(jnp.int32)
        qblk, kblk, vblk, probs = pieces(first)
        vh = vblk.reshape(span, HEADS, -1).astype(jnp.float32)
        out = jnp.einsum('hqk,khd->qhd', lowered(probs), vh)
        return out.astype(jnp.bfloat16).reshape(block, width)
    attn = lax.map(forward_block, jnp.arange(count, dtype=jnp.int32)).reshape(length, width)
    d_attn = jnp.dot(grad_out, w_out.T, preferred_element_type=jnp.float32).astype(jnp.bfloat16)

    def accumulate(total, part, first):
        return lax.dynamic_update_slice_in_dim(total, lax.dynamic_slice_in_dim(total, first, span, 0) + part, first, 0)

    def backward_block(carry, index):
        own_k, own_v, cross_k, cross_v = carry
        first = (index * block).astype(jnp.int32)
        qblk, kblk, vblk, probs = pieces(first)
        qh = qblk.reshape(block, HEADS, -1).astype(jnp.float32)
        kh = kblk.reshape(span, HEADS, -1).astype(jnp.float32)
        vh = vblk.reshape(span, HEADS, -1).astype(jnp.float32)
        do_h = lax.dynamic_slice_in_dim(d_attn, first, block, 0).reshape(block, HEADS, -1).astype(jnp.float32)
        o_h = lax.dynamic_slice_in_dim(attn, first, block, 0).reshape(block, HEADS, -1).astype(jnp.float32)
        delta = lax.optimization_barrier(jnp.sum(do_h * o_h, axis=2))
        dprob = jnp.einsum('qhd,khd->hqk', do_h, vh)
        dscore = lowered(probs * (dprob - delta.T[:, :, None]) * scale)
        grad_q = jnp.einsum('hqk,khd->qhd', dscore, kh).astype(jnp.bfloat16).reshape(block, width)
        part_k = jnp.einsum('hqk,qhd->khd', dscore, qh).reshape(span, width)
        part_v = jnp.einsum('hqk,qhd->khd', lowered(probs), do_h).reshape(span, width)
        shard_start = first // TOK_DEV * TOK_DEV
        pos_k = (first - WINDOW + jnp.arange(span)).astype(jnp.int32)
        cross = (pos_k < shard_start)[:, None]
        zero = jnp.zeros((span, width), jnp.float32)
        own_k = accumulate(own_k, jnp.where(cross, zero, part_k), first)
        own_v = accumulate(own_v, jnp.where(cross, zero, part_v), first)
        cross_k = accumulate(cross_k, jnp.where(cross, part_k, zero), first)
        cross_v = accumulate(cross_v, jnp.where(cross, part_v, zero), first)
        return ((own_k, own_v, cross_k, cross_v), grad_q)
    empty = jnp.zeros((WINDOW + length, width), jnp.float32)
    (own_k, own_v, cross_k, cross_v), grad_qs = lax.scan(backward_block, (empty, empty, empty, empty), jnp.arange(count, dtype=jnp.int32))
    grad_keys = (own_k + lowered(cross_k))[WINDOW:].astype(jnp.bfloat16)
    grad_values = (own_v + lowered(cross_v))[WINDOW:].astype(jnp.bfloat16)
    grad_qkv = jnp.concatenate([grad_qs.reshape(length, width), grad_keys, grad_values], 1)
    grad_normed = jnp.dot(grad_qkv, w_qkv.T, preferred_element_type=jnp.float32)
    scaled = grad_normed * gain
    grad_x = grad_out.astype(jnp.float32) + (scaled - normal_x * lax.optimization_barrier(jnp.mean(scaled * normal_x, axis=1, keepdims=True))) * inv_rms
    term_qkv = lax.dot_general(normed, grad_qkv, (((0,), (0,)), ((), ())), preferred_element_type=jnp.float32)
    return (grad_x.astype(jnp.bfloat16), term_qkv)

def reference(inputs, cotangent, gain, w_qkv, w_out, segment_ids):
    grads = []
    total_qkv = jnp.zeros(w_qkv.shape, jnp.float32)
    for group in range(N_DP):
        grad_x, term_qkv = one_sequence(inputs[group], cotangent[group], gain, w_qkv, w_out, segment_ids[group])
        grads.append(grad_x)
        total_qkv = total_qkv + term_qkv
    return (jnp.stack(grads, 0), total_qkv / N_DP)
```

```python
import functools
import math

import jax
import jax.numpy as jnp
from jax import lax
from jax.experimental import pallas as pl
from jax.experimental.pallas import tpu as pltpu
from jax.sharding import PartitionSpec as P

MESH = pl.DeviceIdType.MESH
F32 = jnp.float32
BF16 = jnp.bfloat16

WINDOW = 512
ROWS = 512
EXT = WINDOW + ROWS
D = 1024
PAIR = 128
PAIRS = D // PAIR
QB = 128
NQ = ROWS // QB
SPAN = WINDOW + QB
TILE = 256
HALF = 256
CHUNKS = 6
EPS = 1e-05
SCALE = 0.125
LOG2E = math.log2(math.e)

NT = (((1,), (1,)), ((), ()))

ORDERS = (
    ("yw", "zu", "yu", "zw", "xw", "xu"),
    ("zw", "yu", "zu", "yw", "xu", "xw"),
    ("yu", "zw", "yw", "zu", "xw", "xu"),
    ("zu", "yw", "zw", "yu", "xu", "xw"),
    ("yw", "zw", "yu", "zu", "xw", "xu"),
    ("zw", "yw", "zu", "yu", "xu", "xw"),
)
STEPS = len(ORDERS[0])
BLOCK = 16
BLOCKS = D // BLOCK


def gray(place):
    return {"u": place // 2, "w": (place // 2 + place) % 2}


def block_places(order):
    places = []
    for block in range(BLOCKS):
        zh, seq = block % 2, block // 2
        at = {"x": seq % 4, "y": seq // 4 % 4, "z": zh * 2 + seq // 16}
        place = 0
        for bit in order:
            place = place * 2 + gray(at[bit[0]])[bit[1]]
        places.append(place)
    return places


def kernel(
    x_hbm,
    cot_hbm,
    gain_ref,
    w_hbm,
    wo_hbm,
    segq_ref,
    segk_ref,
    gx_ref,
    gw_ref,
    x_ref,
    cot_ref,
    w_ref,
    wo_ref,
    xh_ref,
    normed_ref,
    nt_ref,
    q_ref,
    k_ref,
    v_ref,
    kt_ref,
    do_ref,
    mask_ref,
    dq_ref,
    dk_ref,
    dv_ref,
    acck_ref,
    accv_ref,
    back_send,
    back_recv,
    gn_ref,
    own_ref,
    sib_send,
    sib_recv,
    rs_recv,
    gather_ref,
    load_sem,
    halo_sem,
    back_sem,
    sib_sem,
    rs_send_sem,
    rs_recv_sem,
    gather_sem,
):
    s = lax.axis_index("seq")
    d = lax.axis_index("dp")
    x, y, zl = s % 4, s // 4 % 4, s // 16
    core, zh = d % 2, d // 2
    z = zh * 2 + zl

    def device(x, y, z, core):
        return {"seq": z % 2 * 16 + y * 4 + x, "dp": z // 2 * 2 + core}

    nxt = {"seq": (s + 1) % 32, "dp": d}
    prev = {"seq": (s + 31) % 32, "dp": d}

    def flip(place, bit):
        return 3 - place if bit == "u" else place + 1 - 2 * (place % 2)

    partners = {}
    mine = {}
    for axis, place in (("x", x), ("y", y), ("z", z)):
        for bit in "uw":
            at = {"x": x, "y": y, "z": z, axis: flip(place, bit)}
            partners[axis + bit] = device(at["x"], at["y"], at["z"], core)
            mine[axis + bit] = gray(place)[bit]
    sibling = {"seq": s, "dp": zh * 2 + 1 - core}
    others = [
        {"seq": s, "dp": zh * 2 + 1 - core},
        {"seq": s, "dp": (1 - zh) * 2 + core},
        {"seq": s, "dp": (1 - zh) * 2 + 1 - core},
    ]

    loads = []
    for index, (src, dst) in enumerate(
        ((x_hbm, x_ref), (cot_hbm, cot_ref), (wo_hbm, wo_ref), (w_hbm, w_ref))
    ):
        loads.append(pltpu.make_async_copy(src, dst, load_sem.at[index]))
        loads[-1].start()

    barrier = pltpu.get_barrier_semaphore()
    peers = [nxt, prev, *partners.values(), *others]
    for peer in peers:
        pl.semaphore_signal(barrier, inc=1, device_id=peer, device_id_type=MESH)
    pl.semaphore_wait(barrier, len(peers))

    halos = []
    for piece in range(NQ):
        rows = pl.ds(piece * QB, QB)
        halos.append(
            pltpu.make_async_remote_copy(
                src_ref=x_hbm.at[rows],
                dst_ref=xh_ref.at[rows],
                send_sem=halo_sem.at[0, piece],
                recv_sem=halo_sem.at[1, piece],
                device_id=nxt,
                device_id_type=MESH,
            )
        )
    for piece in reversed(range(NQ)):
        halos[piece].start()

    gain = gain_ref[...]

    def norm_rows(src_ref, row, ext_row):
        xf = src_ref[pl.ds(row, QB), :].astype(F32)
        inv = lax.rsqrt(jnp.mean(xf * xf, axis=1, keepdims=True) + EPS)
        normed = (xf * inv * gain).astype(BF16)
        normed_ref[pl.ds(ext_row, QB), :] = normed
        return normed

    loads[0].wait()

    for j in range(NQ):
        normed = norm_rows(x_ref, j * QB, WINDOW + j * QB)
        nt_ref[:, WINDOW + j * QB : WINDOW + (j + 1) * QB] = normed.T

    lane = lax.broadcasted_iota(jnp.int32, (SPAN, QB), 1)
    row = lax.broadcasted_iota(jnp.int32, (SPAN, QB), 0)
    in_window = (row > lane) & (row <= lane + WINDOW)
    for j in range(NQ):
        same = segk_ref[j * QB : j * QB + SPAN, :] == segq_ref[:, j * QB : (j + 1) * QB]
        mask_ref[j] = jnp.where(in_window & same, 0.0, -1e30).astype(F32)

    loads[1].wait()
    loads[2].wait()

    @pl.loop(0, D // TILE)
    def _(n):
        at = pl.ds(pl.multiple_of(n * TILE, TILE), TILE)
        do_ref[:, at] = lax.dot_general(
            cot_ref[...], wo_ref[at, :], NT, preferred_element_type=F32
        ).astype(BF16)

    loads[3].wait()

    def keys_values(first, count):
        @pl.loop(0, D // TILE)
        def _(n):
            at = pl.ds(pl.multiple_of(n * TILE, TILE), TILE)
            at_k = pl.ds(pl.multiple_of(D + n * TILE, TILE), TILE)
            at_v = pl.ds(pl.multiple_of(2 * D + n * TILE, TILE), TILE)
            normed = normed_ref[first : first + count, :]
            k = jnp.dot(normed, w_ref[:, at_k], preferred_element_type=F32).astype(BF16)
            k_ref[first : first + count, at] = k
            kt_ref[at, first : first + count] = k.T
            v = jnp.dot(normed, w_ref[:, at_v], preferred_element_type=F32).astype(BF16)
            v_ref[first : first + count, at] = v

    @pl.loop(0, D // TILE)
    def _(n):
        at = pl.ds(pl.multiple_of(n * TILE, TILE), TILE)
        q_ref[:, at] = jnp.dot(
            normed_ref[WINDOW:, :], w_ref[:, at], preferred_element_type=F32
        ).astype(BF16)

    keys_values(WINDOW, ROWS)

    first_head = lax.broadcasted_iota(jnp.int32, (QB, PAIR), 1) < PAIR // 2
    zero = jnp.zeros((QB, PAIR), BF16)

    def two_heads(block):
        return jnp.concatenate(
            [jnp.where(first_head, block, zero), jnp.where(first_head, zero, block)], 0
        )

    def attend(j, pair):
        at = pl.ds(pl.multiple_of(pair * PAIR, PAIR), PAIR)
        lo = j * QB
        queries = two_heads(q_ref[lo : lo + QB, at])
        grads = two_heads(do_ref[lo : lo + QB, at])
        scores = lax.dot_general(
            k_ref[lo : lo + SPAN, at], queries, NT, preferred_element_type=F32
        )
        dprob = lax.dot_general(
            v_ref[lo : lo + SPAN, at], grads, NT, preferred_element_type=F32
        )
        mask = mask_ref[j]
        scores = scores * (SCALE * LOG2E) + jnp.concatenate([mask, mask], 1)
        expo = jnp.exp2(scores - jnp.max(scores, axis=0, keepdims=True))
        inverse = 1.0 / jnp.sum(expo, axis=0, keepdims=True)
        probs = expo * inverse
        delta = jnp.sum(probs * dprob, axis=0, keepdims=True)
        dscore = (probs * (dprob - delta)).astype(BF16)
        part_v = jnp.dot(probs.astype(BF16), grads, preferred_element_type=F32)
        part_k = jnp.dot(dscore, queries, preferred_element_type=F32)
        dq_t = jnp.dot(kt_ref[at, lo : lo + SPAN], dscore, preferred_element_type=F32)
        dq_t = jnp.concatenate(
            [dq_t[: PAIR // 2, :QB], dq_t[PAIR // 2 :, QB:]], 0
        )
        dq_ref[lo : lo + QB, at] = (dq_t.T * SCALE).astype(BF16)
        fresh = SPAN if j == NQ - 1 else QB
        done = SPAN if j == 0 else QB
        for part, acc_ref, out_ref, scale in (
            (part_v, accv_ref, dv_ref, 1.0),
            (part_k, acck_ref, dk_ref, SCALE),
        ):
            for r in range(0, SPAN, QB):
                value = part[r : r + QB]
                if r >= fresh:
                    value = acc_ref[lo + r : lo + r + QB, at] + value
                if r >= SPAN - done:
                    out_ref[lo + r : lo + r + QB, at] = (value * scale).astype(BF16)
                else:
                    acc_ref[lo + r : lo + r + QB, at] = value

    for j in reversed(range(NQ)):
        halos[j].wait_recv()
        normed = norm_rows(xh_ref, j * QB, j * QB)
        nt_ref[:, j * QB : (j + 1) * QB] = normed.T
        keys_values(j * QB, QB)

        @pl.loop(0, PAIRS // 2)
        def _(p):
            attend(j, p * 2)
            attend(j, p * 2 + 1)

    backs = []
    for n in range(D // TILE):
        at = pl.ds(n * TILE, TILE)
        back_send[n] = (
            lax.dot_general(
                dk_ref[:WINDOW, :], w_ref[at, D : 2 * D], NT, preferred_element_type=F32
            )
            + lax.dot_general(
                dv_ref[:WINDOW, :], w_ref[at, 2 * D :], NT, preferred_element_type=F32
            )
        ).astype(BF16)
        copy = pltpu.make_async_remote_copy(
            src_ref=back_send.at[n],
            dst_ref=back_recv.at[n],
            send_sem=back_sem.at[0, n],
            recv_sem=back_sem.at[1, n],
            device_id=prev,
            device_id_type=MESH,
        )
        copy.start()
        backs.append(copy)

    places = [block_places(order) for order in ORDERS]

    def weight_half(c, half, out_ref):
        part, lo = c // 2, c % 2 * 2 * HALF
        at = pl.ds(pl.multiple_of(lo + half * HALF, HALF), HALF)
        if part == 0:
            value = jnp.dot(
                nt_ref[:, WINDOW:], dq_ref[:, at], preferred_element_type=F32
            )
        else:
            grads = dk_ref if part == 1 else dv_ref
            value = jnp.dot(nt_ref[...], grads[:, at], preferred_element_type=F32)
        value = value.astype(BF16)
        for block, place in enumerate(places[c]):
            out_ref[c, place * BLOCK : (place + 1) * BLOCK, :] = value[
                block * BLOCK : (block + 1) * BLOCK
            ]

    sends = []

    def sibling_copy(c):
        return pltpu.make_async_remote_copy(
            src_ref=sib_send.at[c],
            dst_ref=sib_recv.at[c],
            send_sem=sib_sem.at[0, c],
            recv_sem=sib_sem.at[1, c],
            device_id=sibling,
            device_id_type=MESH,
        )

    def base_of(c, t):
        base = 0
        for i in range(t):
            base = base + mine[ORDERS[c][i]] * (D >> (i + 1))
        return base

    def landing(t):
        return D - (D >> t)

    def halving_copy(c, t):
        length = D >> (t + 1)
        bit = ORDERS[c][t]
        away = pl.multiple_of(base_of(c, t) + (1 - mine[bit]) * length, BLOCK)
        return pltpu.make_async_remote_copy(
            src_ref=own_ref.at[c, pl.ds(away, length)],
            dst_ref=rs_recv.at[c, pl.ds(landing(t), length)],
            send_sem=rs_send_sem.at[c, t],
            recv_sem=rs_recv_sem.at[c, t],
            device_id=partners[bit],
            device_id_type=MESH,
        )

    halvings = {}
    sib_copies = {}

    def add_rows(c, first, src_ref, src_first, length):
        step = min(length, 128)

        @pl.loop(0, length // step)
        def _(i):
            to = pl.ds(pl.multiple_of(first + i * step, BLOCK), step)
            frm = pl.ds(pl.multiple_of(src_first + i * step, BLOCK), step)
            own_ref[c, to, :] = (
                own_ref[c, to, :].astype(F32) + src_ref[c, frm, :].astype(F32)
            ).astype(BF16)

    def stage(c, i):
        if i == 0:
            weight_half(c, 1 - core, sib_send)
            sib_copies[c] = sibling_copy(c)
            sib_copies[c].start()
            weight_half(c, core, own_ref)
        elif i == 1:
            sib_copies[c].wait_recv()
            add_rows(c, 0, sib_recv, 0, D)
            halvings[c, 0] = halving_copy(c, 0)
            halvings[c, 0].start()
        else:
            t = i - 2
            halvings[c, t].wait_recv()
            add_rows(c, base_of(c, t + 1), rs_recv, landing(t), D >> (t + 1))
            if t + 1 < STEPS:
                halvings[c, t + 1] = halving_copy(c, t + 1)
                halvings[c, t + 1].start()

    def own_grad(n):
        at = pl.ds(n * TILE, TILE)
        gn_ref[:, n * TILE : (n + 1) * TILE] = (
            lax.dot_general(dq_ref[...], w_ref[at, :D], NT, preferred_element_type=F32)
            + lax.dot_general(
                dk_ref[WINDOW:, :], w_ref[at, D : 2 * D], NT, preferred_element_type=F32
            )
            + lax.dot_general(
                dv_ref[WINDOW:, :], w_ref[at, 2 * D :], NT, preferred_element_type=F32
            )
        )

    def grad_rows(j):
        rows = slice(j * QB, (j + 1) * QB)
        back = jnp.concatenate([back_recv[n, rows, :] for n in range(D // TILE)], 1)
        xf = x_ref[rows, :].astype(F32)
        inv = lax.rsqrt(jnp.mean(xf * xf, axis=1, keepdims=True) + EPS)
        normal = xf * inv
        scaled = (gn_ref[rows, :] + back.astype(F32)) * gain
        grad = (
            cot_ref[rows, :].astype(F32)
            + (scaled - normal * jnp.mean(scaled * normal, axis=1, keepdims=True)) * inv
        )
        gx_ref[rows, :] = grad.astype(BF16)

    stages = STEPS + 2
    for tick in range(CHUNKS + stages - 1):
        for c in range(CHUNKS):
            if 0 <= tick - c < stages:
                stage(c, tick - c)
        if CHUNKS <= tick < CHUNKS + D // TILE:
            own_grad(tick - CHUNKS)
        if tick == CHUNKS + D // TILE:
            for copy in backs:
                copy.wait_recv()
        if CHUNKS + D // TILE <= tick:
            for j in (2 * (tick - CHUNKS - D // TILE), 2 * (tick - CHUNKS - D // TILE) + 1):
                if j < NQ:
                    grad_rows(j)

    for c in range(CHUNKS):
        rows = pl.ds(pl.multiple_of(base_of(c, STEPS), BLOCK), BLOCK)
        gather_ref[0, :, c * HALF : (c + 1) * HALF] = own_ref[c, rows, :]
    copies = []
    for i, other in enumerate(others):
        copy = pltpu.make_async_remote_copy(
            src_ref=gather_ref.at[0],
            dst_ref=gather_ref.at[i + 1],
            send_sem=gather_sem.at[0, i],
            recv_sem=gather_sem.at[1, i],
            device_id=other,
            device_id_type=MESH,
        )
        copy.start()
        copies.append(copy)
    for i in range(4):
        if i:
            copies[i - 1].wait_recv()
        from_zh = zh if i < 2 else 1 - zh
        from_core = core if i % 2 == 0 else 1 - core
        rows = pl.ds(pl.multiple_of(from_zh * BLOCK, BLOCK), BLOCK)
        for c in range(CHUNKS):
            at = pl.ds(pl.multiple_of(c * 2 * HALF + from_core * HALF, HALF), HALF)
            gw_ref[rows, at] = gather_ref[i, :, c * HALF : (c + 1) * HALF].astype(F32) * 0.25

    for copy in (*halos, *backs, *sib_copies.values(), *halvings.values(), *copies):
        copy.wait_send()


def body(inputs, cotangent, gain, w_qkv, w_out, segment_ids):
    offset = lax.axis_index("seq") * ROWS
    padded = jnp.concatenate([jnp.full((WINDOW,), -1, jnp.int32), segment_ids[0]], 0)
    seg = lax.dynamic_slice_in_dim(padded, offset, EXT, 0)
    any_space = pl.BlockSpec(memory_space=pl.ANY)
    vmem = pl.BlockSpec(memory_space=pltpu.VMEM)
    dma = pltpu.SemaphoreType.DMA
    grad_x, grad_w = pl.pallas_call(
        kernel,
        out_shape=(
            jax.ShapeDtypeStruct((ROWS, D), BF16),
            jax.ShapeDtypeStruct((2 * BLOCK, 3 * D), F32),
        ),
        in_specs=[any_space, any_space, vmem, any_space, any_space, vmem, vmem],
        out_specs=(vmem, vmem),
        scratch_shapes=[
            pltpu.VMEM((ROWS, D), BF16),
            pltpu.VMEM((ROWS, D), BF16),
            pltpu.VMEM((D, 3 * D), BF16),
            pltpu.VMEM((D, D), BF16),
            pltpu.VMEM((WINDOW, D), BF16),
            pltpu.VMEM((EXT, D), BF16),
            pltpu.VMEM((D, EXT), BF16),
            pltpu.VMEM((ROWS, D), BF16),
            pltpu.VMEM((EXT, D), BF16),
            pltpu.VMEM((EXT, D), BF16),
            pltpu.VMEM((D, EXT), BF16),
            pltpu.VMEM((ROWS, D), BF16),
            pltpu.VMEM((NQ, SPAN, QB), F32),
            pltpu.VMEM((ROWS, D), BF16),
            pltpu.VMEM((EXT, D), BF16),
            pltpu.VMEM((EXT, D), BF16),
            pltpu.VMEM((EXT, D), F32),
            pltpu.VMEM((EXT, D), F32),
            pltpu.VMEM((D // TILE, WINDOW, TILE), BF16),
            pltpu.VMEM((D // TILE, WINDOW, TILE), BF16),
            pltpu.VMEM((ROWS, D), F32),
            pltpu.VMEM((CHUNKS, D, HALF), BF16),
            pltpu.VMEM((CHUNKS, D, HALF), BF16),
            pltpu.VMEM((CHUNKS, D, HALF), BF16),
            pltpu.VMEM((CHUNKS, D, HALF), BF16),
            pltpu.VMEM((4, BLOCK, CHUNKS * HALF), BF16),
            dma((4,)),
            dma((2, NQ)),
            dma((2, D // TILE)),
            dma((2, CHUNKS)),
            dma((CHUNKS, STEPS)),
            dma((CHUNKS, STEPS)),
            dma((2, 3)),
        ],
        compiler_params=pltpu.CompilerParams(
            collective_id=0, has_side_effects=True, vmem_limit_bytes=60 * 1024 * 1024
        ),
    )(
        inputs[0],
        cotangent[0],
        gain[None],
        w_qkv,
        w_out,
        seg[None, WINDOW:],
        seg[:, None],
    )
    return grad_x[None], grad_w


def solution(mesh):
    return jax.shard_map(
        body,
        mesh=mesh,
        in_specs=(P("dp", "seq", None), P("dp", "seq", None), P(), P(), P(), P("dp", None)),
        out_specs=(P("dp", "seq", None), P("seq", None)),
        check_vma=False,
    )
```

```python
import functools
import math

import jax
import jax.numpy as jnp
from jax import lax
from jax.experimental import pallas as pl
from jax.experimental.pallas import tpu as pltpu
from jax.sharding import PartitionSpec as P

MESH = pl.DeviceIdType.MESH
F32 = jnp.float32
BF16 = jnp.bfloat16

WINDOW = 512
ROWS = 512
EXT = WINDOW + ROWS
D = 1024
PAIR = 128
PAIRS = D // PAIR
QB = 128
NQ = ROWS // QB
SPAN = WINDOW + QB
TILE = 256
HALF = 256
CHUNKS = 6
EPS = 1e-05
SCALE = 0.125
LOG2E = math.log2(math.e)

NT = (((1,), (1,)), ((), ()))

ORDERS = (
    ("yw", "zu", "yu", "zw", "xw", "xu"),
    ("zw", "yu", "zu", "yw", "xu", "xw"),
    ("yu", "zw", "yw", "zu", "xw", "xu"),
    ("zu", "yw", "zw", "yu", "xu", "xw"),
    ("xw", "zu", "yw", "xu", "yu", "zw"),
    ("xu", "yw", "zu", "xw", "zw", "yu"),
)
STEPS = len(ORDERS[0])
SEQUENCE = (3, 0, 1, 2)
BLOCK = 16
BLOCKS = D // BLOCK


def gray(place):
    return {"u": place // 2, "w": (place // 2 + place) % 2}


def block_places(order):
    places = []
    for block in range(BLOCKS):
        zh, seq = block % 2, block // 2
        at = {"x": seq % 4, "y": seq // 4 % 4, "z": zh * 2 + seq // 16}
        place = 0
        for bit in order:
            place = place * 2 + gray(at[bit[0]])[bit[1]]
        places.append(place)
    return places


def kernel(
    x_hbm,
    cot_hbm,
    gain_ref,
    w_hbm,
    wo_hbm,
    segq_ref,
    segk_ref,
    gx_ref,
    gw_ref,
    x_ref,
    cot_ref,
    w_ref,
    wo_ref,
    xh_ref,
    normed_ref,
    nt_ref,
    q_ref,
    k_ref,
    v_ref,
    kt_ref,
    do_ref,
    mask_ref,
    dq_ref,
    dk_ref,
    dv_ref,
    acck_ref,
    accv_ref,
    back_send,
    back_recv,
    gn_ref,
    own_ref,
    sib_send,
    sib_recv,
    rs_recv,
    gather_ref,
    load_sem,
    halo_sem,
    back_sem,
    sib_sem,
    rs_send_sem,
    rs_recv_sem,
    gather_sem,
):
    s = lax.axis_index("seq")
    d = lax.axis_index("dp")
    x, y, zl = s % 4, s // 4 % 4, s // 16
    core, zh = d % 2, d // 2
    z = zh * 2 + zl

    def device(x, y, z, core):
        return {"seq": z % 2 * 16 + y * 4 + x, "dp": z // 2 * 2 + core}

    nxt = {"seq": (s + 1) % 32, "dp": d}
    prev = {"seq": (s + 31) % 32, "dp": d}

    def flip(place, bit):
        return 3 - place if bit == "u" else place + 1 - 2 * (place % 2)

    partners = {}
    mine = {}
    for axis, place in (("x", x), ("y", y), ("z", z)):
        for bit in "uw":
            at = {"x": x, "y": y, "z": z, axis: flip(place, bit)}
            partners[axis + bit] = device(at["x"], at["y"], at["z"], core)
            mine[axis + bit] = gray(place)[bit]
    sibling = {"seq": s, "dp": zh * 2 + 1 - core}
    others = [
        {"seq": s, "dp": zh * 2 + 1 - core},
        {"seq": s, "dp": (1 - zh) * 2 + core},
        {"seq": s, "dp": (1 - zh) * 2 + 1 - core},
    ]

    loads = []
    for index, (src, dst) in enumerate(
        ((x_hbm, x_ref), (cot_hbm, cot_ref), (wo_hbm, wo_ref), (w_hbm, w_ref))
    ):
        loads.append(pltpu.make_async_copy(src, dst, load_sem.at[index]))
        loads[-1].start()

    barrier = pltpu.get_barrier_semaphore()
    peers = [nxt, prev, *partners.values(), *others]
    for peer in peers:
        pl.semaphore_signal(barrier, inc=1, device_id=peer, device_id_type=MESH)
    pl.semaphore_wait(barrier, len(peers))

    halos = []
    for piece in range(NQ):
        rows = pl.ds(piece * QB, QB)
        halos.append(
            pltpu.make_async_remote_copy(
                src_ref=x_hbm.at[rows],
                dst_ref=xh_ref.at[rows],
                send_sem=halo_sem.at[0, piece],
                recv_sem=halo_sem.at[1, piece],
                device_id=nxt,
                device_id_type=MESH,
            )
        )
    for piece in SEQUENCE:
        halos[piece].start()

    gain = gain_ref[...]

    def norm_rows(src_ref, row, ext_row):
        xf = src_ref[pl.ds(row, QB), :].astype(F32)
        inv = lax.rsqrt(jnp.mean(xf * xf, axis=1, keepdims=True) + EPS)
        normed = (xf * inv * gain).astype(BF16)
        normed_ref[pl.ds(ext_row, QB), :] = normed
        return normed

    loads[0].wait()

    for j in range(NQ):
        normed = norm_rows(x_ref, j * QB, WINDOW + j * QB)
        nt_ref[:, WINDOW + j * QB : WINDOW + (j + 1) * QB] = normed.T

    lane = lax.broadcasted_iota(jnp.int32, (SPAN, QB), 1)
    row = lax.broadcasted_iota(jnp.int32, (SPAN, QB), 0)
    in_window = (row > lane) & (row <= lane + WINDOW)
    for j in range(NQ):
        same = segk_ref[j * QB : j * QB + SPAN, :] == segq_ref[:, j * QB : (j + 1) * QB]
        mask_ref[j] = jnp.where(in_window & same, 0.0, -1e30).astype(F32)

    loads[1].wait()
    loads[2].wait()

    @pl.loop(0, D // TILE)
    def _(n):
        at = pl.ds(pl.multiple_of(n * TILE, TILE), TILE)
        do_ref[:, at] = lax.dot_general(
            cot_ref[...], wo_ref[at, :], NT, preferred_element_type=F32
        ).astype(BF16)

    loads[3].wait()

    def keys_values(first, count):
        @pl.loop(0, D // TILE)
        def _(n):
            at = pl.ds(pl.multiple_of(n * TILE, TILE), TILE)
            at_k = pl.ds(pl.multiple_of(D + n * TILE, TILE), TILE)
            at_v = pl.ds(pl.multiple_of(2 * D + n * TILE, TILE), TILE)
            normed = normed_ref[first : first + count, :]
            k = jnp.dot(normed, w_ref[:, at_k], preferred_element_type=F32).astype(BF16)
            k_ref[first : first + count, at] = k
            kt_ref[at, first : first + count] = k.T
            v = jnp.dot(normed, w_ref[:, at_v], preferred_element_type=F32).astype(BF16)
            v_ref[first : first + count, at] = v

    @pl.loop(0, D // TILE)
    def _(n):
        at = pl.ds(pl.multiple_of(n * TILE, TILE), TILE)
        q_ref[:, at] = jnp.dot(
            normed_ref[WINDOW:, :], w_ref[:, at], preferred_element_type=F32
        ).astype(BF16)

    keys_values(WINDOW, ROWS)

    first_head = lax.broadcasted_iota(jnp.int32, (QB, PAIR), 1) < PAIR // 2
    zero = jnp.zeros((QB, PAIR), BF16)

    def two_heads(block):
        return jnp.concatenate(
            [jnp.where(first_head, block, zero), jnp.where(first_head, zero, block)], 0
        )

    def attend(j, pair):
        at = pl.ds(pl.multiple_of(pair * PAIR, PAIR), PAIR)
        lo = j * QB
        queries = two_heads(q_ref[lo : lo + QB, at])
        grads = two_heads(do_ref[lo : lo + QB, at])
        scores = lax.dot_general(
            k_ref[lo : lo + SPAN, at], queries, NT, preferred_element_type=F32
        )
        dprob = lax.dot_general(
            v_ref[lo : lo + SPAN, at], grads, NT, preferred_element_type=F32
        )
        mask = mask_ref[j]
        scores = scores * (SCALE * LOG2E) + jnp.concatenate([mask, mask], 1)
        expo = jnp.exp2(scores - jnp.max(scores, axis=0, keepdims=True))
        inverse = 1.0 / jnp.sum(expo, axis=0, keepdims=True)
        probs = expo * inverse
        delta = jnp.sum(probs * dprob, axis=0, keepdims=True)
        dscore = (probs * (dprob - delta)).astype(BF16)
        part_v = jnp.dot(probs.astype(BF16), grads, preferred_element_type=F32)
        part_k = jnp.dot(dscore, queries, preferred_element_type=F32)
        dq_t = jnp.dot(kt_ref[at, lo : lo + SPAN], dscore, preferred_element_type=F32)
        dq_t = jnp.concatenate(
            [dq_t[: PAIR // 2, :QB], dq_t[PAIR // 2 :, QB:]], 0
        )
        dq_ref[lo : lo + QB, at] = (dq_t.T * SCALE).astype(BF16)
        for r in range(0, SPAN, QB):
            block = (lo + r) // QB
            reached = [i for i in SEQUENCE if i <= block <= i + SPAN // QB - 1]
            rows = slice(lo + r, lo + r + QB)
            for part, acc_ref, out_ref, scale in (
                (part_v, accv_ref, dv_ref, 1.0),
                (part_k, acck_ref, dk_ref, SCALE),
            ):
                value = part[r : r + QB]
                if j != reached[0]:
                    value = acc_ref[rows, at] + value
                if j == reached[-1]:
                    out_ref[rows, at] = (value * scale).astype(BF16)
                else:
                    acc_ref[rows, at] = value

    def arrive(j):
        halos[j].wait_recv()
        normed = norm_rows(xh_ref, j * QB, j * QB)
        nt_ref[:, j * QB : (j + 1) * QB] = normed.T
        keys_values(j * QB, QB)

    backs = {}

    def give_back(b):
        rows = slice(b * QB, (b + 1) * QB)

        @pl.loop(0, D // TILE)
        def _(n):
            at = pl.ds(pl.multiple_of(n * TILE, TILE), TILE)
            back_send[b, :, at] = (
                lax.dot_general(
                    dk_ref[rows, :], w_ref[at, D : 2 * D], NT, preferred_element_type=F32
                )
                + lax.dot_general(
                    dv_ref[rows, :], w_ref[at, 2 * D :], NT, preferred_element_type=F32
                )
            ).astype(BF16)

        backs[b] = pltpu.make_async_remote_copy(
            src_ref=back_send.at[b],
            dst_ref=back_recv.at[b],
            send_sem=back_sem.at[0, b],
            recv_sem=back_sem.at[1, b],
            device_id=prev,
            device_id_type=MESH,
        )
        backs[b].start()

    arrived = set()
    for step, j in enumerate(SEQUENCE):
        for piece in SEQUENCE:
            if piece >= j and piece not in arrived:
                arrived.add(piece)
                arrive(piece)

        @pl.loop(0, PAIRS // 2)
        def _(p):
            attend(j, p * 2)
            attend(j, p * 2 + 1)

        for b in range(NQ):
            if all(i in SEQUENCE[: step + 1] for i in range(b + 1)) and b not in backs:
                give_back(b)

    places = [block_places(order) for order in ORDERS]

    def weight_half(c, half, out_ref, add_ref=None):
        part, lo = c // 2, c % 2 * 2 * HALF
        at = pl.ds(pl.multiple_of(lo + half * HALF, HALF), HALF)
        if part == 0:
            value = jnp.dot(
                nt_ref[:, WINDOW:], dq_ref[:, at], preferred_element_type=F32
            )
        else:
            grads = dk_ref if part == 1 else dv_ref
            value = jnp.dot(nt_ref[...], grads[:, at], preferred_element_type=F32)
        for block, place in enumerate(places[c]):
            rows = slice(place * BLOCK, (place + 1) * BLOCK)
            piece = value[block * BLOCK : (block + 1) * BLOCK]
            if add_ref is not None:
                piece = piece + add_ref[c, rows, :].astype(F32)
            out_ref[c, rows, :] = piece.astype(BF16)

    def sibling_copy(c):
        return pltpu.make_async_remote_copy(
            src_ref=sib_send.at[c],
            dst_ref=sib_recv.at[c],
            send_sem=sib_sem.at[0, c],
            recv_sem=sib_sem.at[1, c],
            device_id=sibling,
            device_id_type=MESH,
        )

    def base_of(c, t):
        base = 0
        for i in range(t):
            base = base + mine[ORDERS[c][i]] * (D >> (i + 1))
        return base

    def landing(t):
        return D - (D >> t)

    def halving_copy(c, t):
        length = D >> (t + 1)
        bit = ORDERS[c][t]
        away = pl.multiple_of(base_of(c, t) + (1 - mine[bit]) * length, BLOCK)
        return pltpu.make_async_remote_copy(
            src_ref=own_ref.at[c, pl.ds(away, length)],
            dst_ref=rs_recv.at[c, pl.ds(landing(t), length)],
            send_sem=rs_send_sem.at[c, t],
            recv_sem=rs_recv_sem.at[c, t],
            device_id=partners[bit],
            device_id_type=MESH,
        )

    halvings = {}
    sib_copies = {}

    def add_rows(c, first, src_ref, src_first, length):
        step = min(length, 128)

        @pl.loop(0, length // step)
        def _(i):
            to = pl.ds(pl.multiple_of(first + i * step, BLOCK), step)
            frm = pl.ds(pl.multiple_of(src_first + i * step, BLOCK), step)
            own_ref[c, to, :] = (
                own_ref[c, to, :].astype(F32) + src_ref[c, frm, :].astype(F32)
            ).astype(BF16)

    def stage(c, t):
        halvings[c, t].wait_recv()
        add_rows(c, base_of(c, t + 1), rs_recv, landing(t), D >> (t + 1))
        if t + 1 < STEPS:
            halvings[c, t + 1] = halving_copy(c, t + 1)
            halvings[c, t + 1].start()

    def own_grad(n):
        at = pl.ds(n * TILE, TILE)
        gn_ref[:, n * TILE : (n + 1) * TILE] = (
            lax.dot_general(dq_ref[...], w_ref[at, :D], NT, preferred_element_type=F32)
            + lax.dot_general(
                dk_ref[WINDOW:, :], w_ref[at, D : 2 * D], NT, preferred_element_type=F32
            )
            + lax.dot_general(
                dv_ref[WINDOW:, :], w_ref[at, 2 * D :], NT, preferred_element_type=F32
            )
        )

    def grad_rows(j):
        rows = slice(j * QB, (j + 1) * QB)
        xf = x_ref[rows, :].astype(F32)
        inv = lax.rsqrt(jnp.mean(xf * xf, axis=1, keepdims=True) + EPS)
        normal = xf * inv
        scaled = (gn_ref[rows, :] + back_recv[j].astype(F32)) * gain
        grad = (
            cot_ref[rows, :].astype(F32)
            + (scaled - normal * jnp.mean(scaled * normal, axis=1, keepdims=True)) * inv
        )
        gx_ref[rows, :] = grad.astype(BF16)

    for c in range(CHUNKS):
        weight_half(c, 1 - core, sib_send)
        sib_copies[c] = sibling_copy(c)
        sib_copies[c].start()
    for c in range(CHUNKS):
        sib_copies[c].wait_recv()
        weight_half(c, core, own_ref, sib_recv)
        halvings[c, 0] = halving_copy(c, 0)
        halvings[c, 0].start()
    for n in range(D // TILE):
        own_grad(n)
    for t in range(STEPS):
        for c in range(CHUNKS):
            stage(c, t)
        if t < NQ:
            backs[t].wait_recv()
            grad_rows(t)

    for c in range(CHUNKS):
        rows = pl.ds(pl.multiple_of(base_of(c, STEPS), BLOCK), BLOCK)
        gather_ref[0, :, c * HALF : (c + 1) * HALF] = own_ref[c, rows, :]
    copies = []
    for i, other in enumerate(others):
        copy = pltpu.make_async_remote_copy(
            src_ref=gather_ref.at[0],
            dst_ref=gather_ref.at[i + 1],
            send_sem=gather_sem.at[0, i],
            recv_sem=gather_sem.at[1, i],
            device_id=other,
            device_id_type=MESH,
        )
        copy.start()
        copies.append(copy)
    for i in range(4):
        if i:
            copies[i - 1].wait_recv()
        from_zh = zh if i < 2 else 1 - zh
        from_core = core if i % 2 == 0 else 1 - core
        rows = pl.ds(pl.multiple_of(from_zh * BLOCK, BLOCK), BLOCK)
        for c in range(CHUNKS):
            at = pl.ds(pl.multiple_of(c * 2 * HALF + from_core * HALF, HALF), HALF)
            gw_ref[rows, at] = gather_ref[i, :, c * HALF : (c + 1) * HALF].astype(F32) * 0.25

    for copy in (*halos, *backs.values(), *sib_copies.values(), *halvings.values(), *copies):
        copy.wait_send()


def body(inputs, cotangent, gain, w_qkv, w_out, segment_ids):
    offset = lax.axis_index("seq") * ROWS
    padded = jnp.concatenate([jnp.full((WINDOW,), -1, jnp.int32), segment_ids[0]], 0)
    seg = lax.dynamic_slice_in_dim(padded, offset, EXT, 0)
    any_space = pl.BlockSpec(memory_space=pl.ANY)
    vmem = pl.BlockSpec(memory_space=pltpu.VMEM)
    dma = pltpu.SemaphoreType.DMA
    grad_x, grad_w = pl.pallas_call(
        kernel,
        out_shape=(
            jax.ShapeDtypeStruct((ROWS, D), BF16),
            jax.ShapeDtypeStruct((2 * BLOCK, 3 * D), F32),
        ),
        in_specs=[any_space, any_space, vmem, any_space, any_space, vmem, vmem],
        out_specs=(vmem, vmem),
        scratch_shapes=[
            pltpu.VMEM((ROWS, D), BF16),
            pltpu.VMEM((ROWS, D), BF16),
            pltpu.VMEM((D, 3 * D), BF16),
            pltpu.VMEM((D, D), BF16),
            pltpu.VMEM((WINDOW, D), BF16),
            pltpu.VMEM((EXT, D), BF16),
            pltpu.VMEM((D, EXT), BF16),
            pltpu.VMEM((ROWS, D), BF16),
            pltpu.VMEM((EXT, D), BF16),
            pltpu.VMEM((EXT, D), BF16),
            pltpu.VMEM((D, EXT), BF16),
            pltpu.VMEM((ROWS, D), BF16),
            pltpu.VMEM((NQ, SPAN, QB), F32),
            pltpu.VMEM((ROWS, D), BF16),
            pltpu.VMEM((EXT, D), BF16),
            pltpu.VMEM((EXT, D), BF16),
            pltpu.VMEM((EXT, D), F32),
            pltpu.VMEM((EXT, D), F32),
            pltpu.VMEM((NQ, QB, D), BF16),
            pltpu.VMEM((NQ, QB, D), BF16),
            pltpu.VMEM((ROWS, D), F32),
            pltpu.VMEM((CHUNKS, D, HALF), BF16),
            pltpu.VMEM((CHUNKS, D, HALF), BF16),
            pltpu.VMEM((CHUNKS, D, HALF), BF16),
            pltpu.VMEM((CHUNKS, D, HALF), BF16),
            pltpu.VMEM((4, BLOCK, CHUNKS * HALF), BF16),
            dma((4,)),
            dma((2, NQ)),
            dma((2, NQ)),
            dma((2, CHUNKS)),
            dma((CHUNKS, STEPS)),
            dma((CHUNKS, STEPS)),
            dma((2, 3)),
        ],
        compiler_params=pltpu.CompilerParams(
            collective_id=0, has_side_effects=True, vmem_limit_bytes=60 * 1024 * 1024
        ),
    )(
        inputs[0],
        cotangent[0],
        gain[None],
        w_qkv,
        w_out,
        seg[None, WINDOW:],
        seg[:, None],
    )
    return grad_x[None], grad_w


def solution(mesh):
    return jax.shard_map(
        body,
        mesh=mesh,
        in_specs=(P("dp", "seq", None), P("dp", "seq", None), P(), P(), P(), P("dp", None)),
        out_specs=(P("dp", "seq", None), P("seq", None)),
        check_vma=False,
    )
```

```python
import functools
import math

import jax
import jax.numpy as jnp
from jax import lax
from jax.experimental import pallas as pl
from jax.experimental.pallas import tpu as pltpu
from jax.sharding import PartitionSpec as P

MESH = pl.DeviceIdType.MESH
F32 = jnp.float32
BF16 = jnp.bfloat16

WINDOW = 512
ROWS = 512
EXT = WINDOW + ROWS
D = 1024
PAIR = 128
PAIRS = D // PAIR
QB = 128
NQ = ROWS // QB
SPAN = WINDOW + QB
TILE = 256
HALF = 256
CHUNKS = 6
EPS = 1e-05
SCALE = 0.125
LOG2E = math.log2(math.e)

NT = (((1,), (1,)), ((), ()))

ORDERS = (
    ("zw", "yw", "zu", "yu", "xw", "xu"),
    ("zu", "yu", "zw", "yw", "xu", "xw"),
    ("zw", "xw", "zu", "xu", "yw", "yu"),
    ("zu", "xu", "zw", "xw", "yu", "yw"),
    ("yw", "zw", "yu", "zu", "xw", "xu"),
    ("yu", "zu", "yw", "zw", "xu", "xw"),
)
STEPS = len(ORDERS[0])
SEQUENCE = (3, 2, 0, 1)
RETURNS = {0: (0, 1), 1: (1, 3)}
BLOCK = 16
BLOCKS = D // BLOCK


def gray(place):
    return {"u": place // 2, "w": (place // 2 + place) % 2}


def block_places(order):
    places = []
    for block in range(BLOCKS):
        zh, seq = block % 2, block // 2
        at = {"x": seq % 4, "y": seq // 4 % 4, "z": zh * 2 + seq // 16}
        place = 0
        for bit in order:
            place = place * 2 + gray(at[bit[0]])[bit[1]]
        places.append(place)
    return places


def kernel(
    x_hbm,
    cot_hbm,
    gain_ref,
    w_hbm,
    wo_hbm,
    segq_ref,
    segk_ref,
    gx_ref,
    gw_ref,
    x_ref,
    cot_ref,
    w_ref,
    wo_ref,
    xh_ref,
    normed_ref,
    nt_ref,
    q_ref,
    k_ref,
    v_ref,
    kt_ref,
    do_ref,
    mask_ref,
    dq_ref,
    dk_ref,
    dv_ref,
    acck_ref,
    accv_ref,
    expo_ref,
    dprob_ref,
    probs_a,
    dscore_a,
    probs_b,
    dscore_b,
    back_send,
    back_recv,
    own_ref,
    sib_recv,
    rs_recv,
    gather_ref,
    load_sem,
    halo_sem,
    back_sem,
    sib_sem,
    rs_send_sem,
    rs_recv_sem,
    gather_sem,
):
    s = lax.axis_index("seq")
    d = lax.axis_index("dp")
    x, y, zl = s % 4, s // 4 % 4, s // 16
    core, zh = d % 2, d // 2
    z = zh * 2 + zl

    def device(x, y, z, core):
        return {"seq": z % 2 * 16 + y * 4 + x, "dp": z // 2 * 2 + core}

    nxt = {"seq": (s + 1) % 32, "dp": d}
    prev = {"seq": (s + 31) % 32, "dp": d}

    def flip(place, bit):
        return 3 - place if bit == "u" else place + 1 - 2 * (place % 2)

    partners = {}
    mine = {}
    for axis, place in (("x", x), ("y", y), ("z", z)):
        for bit in "uw":
            at = {"x": x, "y": y, "z": z, axis: flip(place, bit)}
            partners[axis + bit] = device(at["x"], at["y"], at["z"], core)
            mine[axis + bit] = gray(place)[bit]
    sibling = {"seq": s, "dp": zh * 2 + 1 - core}
    others = [
        {"seq": s, "dp": zh * 2 + 1 - core},
        {"seq": s, "dp": (1 - zh) * 2 + core},
        {"seq": s, "dp": (1 - zh) * 2 + 1 - core},
    ]

    loads = []
    for index, (src, dst) in enumerate(
        ((x_hbm, x_ref), (cot_hbm, cot_ref), (wo_hbm, wo_ref), (w_hbm, w_ref))
    ):
        loads.append(pltpu.make_async_copy(src, dst, load_sem.at[index]))
        loads[-1].start()

    barrier = pltpu.get_barrier_semaphore()
    peers = [nxt, prev, *partners.values(), *others]
    for peer in peers:
        pl.semaphore_signal(barrier, inc=1, device_id=peer, device_id_type=MESH)
    pl.semaphore_wait(barrier, len(peers))

    halos = []
    for piece in range(NQ):
        rows = pl.ds(piece * QB, QB)
        halos.append(
            pltpu.make_async_remote_copy(
                src_ref=x_hbm.at[rows],
                dst_ref=xh_ref.at[rows],
                send_sem=halo_sem.at[0, piece],
                recv_sem=halo_sem.at[1, piece],
                device_id=nxt,
                device_id_type=MESH,
            )
        )
    for piece in reversed(range(NQ)):
        halos[piece].start()

    gain = gain_ref[...]

    def norm_rows(src_ref, row, ext_row):
        xf = src_ref[pl.ds(row, QB), :].astype(F32)
        inv = lax.rsqrt(jnp.mean(xf * xf, axis=1, keepdims=True) + EPS)
        normed = (xf * inv * gain).astype(BF16)
        normed_ref[pl.ds(ext_row, QB), :] = normed
        return normed

    loads[0].wait()

    for j in range(NQ):
        normed = norm_rows(x_ref, j * QB, WINDOW + j * QB)
        nt_ref[:, WINDOW + j * QB : WINDOW + (j + 1) * QB] = normed.T

    lane = lax.broadcasted_iota(jnp.int32, (SPAN, QB), 1)
    row = lax.broadcasted_iota(jnp.int32, (SPAN, QB), 0)
    in_window = (row > lane) & (row <= lane + WINDOW)
    for j in range(NQ):
        same = segk_ref[j * QB : j * QB + SPAN, :] == segq_ref[:, j * QB : (j + 1) * QB]
        mask_ref[j] = jnp.where(in_window & same, 0.0, -1e30).astype(F32)

    loads[1].wait()
    loads[2].wait()

    @pl.loop(0, D // TILE)
    def _(n):
        at = pl.ds(pl.multiple_of(n * TILE, TILE), TILE)
        do_ref[:, at] = lax.dot_general(
            cot_ref[...], wo_ref[at, :], NT, preferred_element_type=F32
        ).astype(BF16)

    loads[3].wait()

    def keys_values(first, count):
        @pl.loop(0, D // TILE)
        def _(n):
            at = pl.ds(pl.multiple_of(n * TILE, TILE), TILE)
            at_k = pl.ds(pl.multiple_of(D + n * TILE, TILE), TILE)
            at_v = pl.ds(pl.multiple_of(2 * D + n * TILE, TILE), TILE)
            normed = normed_ref[first : first + count, :]
            k = jnp.dot(normed, w_ref[:, at_k], preferred_element_type=F32).astype(BF16)
            k_ref[first : first + count, at] = k
            kt_ref[at, first : first + count] = k.T
            v = jnp.dot(normed, w_ref[:, at_v], preferred_element_type=F32).astype(BF16)
            v_ref[first : first + count, at] = v

    @pl.loop(0, D // TILE)
    def _(n):
        at = pl.ds(pl.multiple_of(n * TILE, TILE), TILE)
        q_ref[:, at] = jnp.dot(
            normed_ref[WINDOW:, :], w_ref[:, at], preferred_element_type=F32
        ).astype(BF16)

    keys_values(WINDOW, ROWS)

    first_head = lax.broadcasted_iota(jnp.int32, (QB, PAIR), 1) < PAIR // 2
    zero = jnp.zeros((QB, PAIR), BF16)

    def two_heads(block):
        return jnp.concatenate(
            [jnp.where(first_head, block, zero), jnp.where(first_head, zero, block)], 0
        )

    def scores_of(j, pair, held):
        at = pl.ds(pl.multiple_of(pair * PAIR, PAIR), PAIR)
        span = slice(j * QB, j * QB + SPAN)
        probs_ref, dscore_ref = held
        state = {}

        def scores():
            queries = two_heads(q_ref[j * QB : (j + 1) * QB, at])
            value = lax.dot_general(k_ref[span, at], queries, NT, preferred_element_type=F32)
            mask = mask_ref[j]
            value = value * (SCALE * LOG2E) + jnp.concatenate([mask, mask], 1)
            expo_ref[...] = value
            state["top"] = jnp.max(value, axis=0, keepdims=True)

        def sums():
            grads = two_heads(do_ref[j * QB : (j + 1) * QB, at])
            expo = jnp.exp2(expo_ref[...] - state["top"])
            dprob = lax.dot_general(v_ref[span, at], grads, NT, preferred_element_type=F32)
            expo_ref[...] = expo
            dprob_ref[...] = dprob
            state["inverse"] = 1.0 / jnp.sum(expo, axis=0, keepdims=True)
            total = jnp.sum(expo * dprob, axis=0, keepdims=True)
            state["delta"] = total * state["inverse"]

        def products():
            probs = expo_ref[...] * state["inverse"]
            probs_ref[...] = probs.astype(BF16)
            dscore_ref[...] = (probs * (dprob_ref[...] - state["delta"])).astype(BF16)

        return [scores, sums, products]

    def grads_of(j, pair, held):
        at = pl.ds(pl.multiple_of(pair * PAIR, PAIR), PAIR)
        lo = j * QB
        probs_ref, dscore_ref = held

        def add_up(part, acc_ref, out_ref, scale):
            for r in range(0, SPAN, QB):
                block = (lo + r) // QB
                reached = [i for i in SEQUENCE if i <= block <= i + SPAN // QB - 1]
                rows = slice(lo + r, lo + r + QB)
                value = part[r : r + QB]
                if j != reached[0]:
                    value = acc_ref[rows, at] + value
                if j == reached[-1]:
                    out_ref[rows, at] = (value * scale).astype(BF16)
                else:
                    acc_ref[rows, at] = value

        def values():
            grads = two_heads(do_ref[lo : lo + QB, at])
            part = jnp.dot(probs_ref[...], grads, preferred_element_type=F32)
            add_up(part, accv_ref, dv_ref, 1.0)

        def keys():
            queries = two_heads(q_ref[lo : lo + QB, at])
            part = jnp.dot(dscore_ref[...], queries, preferred_element_type=F32)
            add_up(part, acck_ref, dk_ref, SCALE)

        def queries():
            part = jnp.dot(
                kt_ref[at, lo : lo + SPAN], dscore_ref[...], preferred_element_type=F32
            )
            part = jnp.concatenate([part[: PAIR // 2, :QB], part[PAIR // 2 :, QB:]], 0)
            dq_ref[lo : lo + QB, at] = (part.T * SCALE).astype(BF16)

        return [values, keys, queries]

    def side_by_side(one, other):
        for i in range(3):
            for steps in (one, other):
                if steps:
                    steps[i]()

    def arrive(j):
        halos[j].wait_recv()
        normed = norm_rows(xh_ref, j * QB, j * QB)
        nt_ref[:, j * QB : (j + 1) * QB] = normed.T
        keys_values(j * QB, QB)

    backs = {}

    def give_back(first, count):
        rows = slice(first * QB, (first + count) * QB)

        @pl.loop(0, D // TILE)
        def _(n):
            at = pl.ds(pl.multiple_of(n * TILE, TILE), TILE)
            value = (
                lax.dot_general(
                    dk_ref[rows, :], w_ref[at, D : 2 * D], NT, preferred_element_type=F32
                )
                + lax.dot_general(
                    dv_ref[rows, :], w_ref[at, 2 * D :], NT, preferred_element_type=F32
                )
            ).astype(BF16)
            for i in range(count):
                back_send[first + i, :, at] = value[i * QB : (i + 1) * QB]

        for b in range(first, first + count):
            backs[b] = pltpu.make_async_remote_copy(
                src_ref=back_send.at[b],
                dst_ref=back_recv.at[b],
                send_sem=back_sem.at[0, b],
                recv_sem=back_sem.at[1, b],
                device_id=prev,
                device_id_type=MESH,
            )
            backs[b].start()

    even, odd = (probs_a, dscore_a), (probs_b, dscore_b)
    last = None
    arrived = set()
    for j in SEQUENCE:
        for piece in reversed(range(j, NQ)):
            if piece not in arrived:
                arrived.add(piece)
                arrive(piece)
        side_by_side(scores_of(j, 0, even), last and grads_of(*last))
        if last and last[0] in RETURNS:
            give_back(*RETURNS[last[0]])
        side_by_side(scores_of(j, 1, odd), grads_of(j, 0, even))

        @pl.loop(1, PAIRS // 2)
        def _(p):
            side_by_side(scores_of(j, p * 2, even), grads_of(j, p * 2 - 1, odd))
            side_by_side(scores_of(j, p * 2 + 1, odd), grads_of(j, p * 2, even))

        last = (j, PAIRS - 1, odd)
    side_by_side(None, grads_of(*last))
    give_back(*RETURNS[last[0]])

    places = [block_places(order) for order in ORDERS]
    sib_send = [
        ref.at[:, i * HALF : (i + 1) * HALF] for ref in (k_ref, v_ref) for i in range(D // HALF)
    ]

    def weight_half(c, half, out_ref, add_ref=None):
        part, lo = c // 2, c % 2 * 2 * HALF
        at = pl.ds(pl.multiple_of(lo + half * HALF, HALF), HALF)
        if part == 0:
            value = jnp.dot(
                nt_ref[:, WINDOW:], dq_ref[:, at], preferred_element_type=F32
            )
        else:
            grads = dk_ref if part == 1 else dv_ref
            value = jnp.dot(nt_ref[...], grads[:, at], preferred_element_type=F32)
        for block, place in enumerate(places[c]):
            rows = slice(place * BLOCK, (place + 1) * BLOCK)
            piece = value[block * BLOCK : (block + 1) * BLOCK]
            if add_ref is not None:
                piece = piece + add_ref[rows, :].astype(F32)
            out_ref[rows, :] = piece.astype(BF16)

    def sibling_copy(c):
        return pltpu.make_async_remote_copy(
            src_ref=sib_send[c],
            dst_ref=sib_recv.at[c],
            send_sem=sib_sem.at[0, c],
            recv_sem=sib_sem.at[1, c],
            device_id=sibling,
            device_id_type=MESH,
        )

    def base_of(c, t):
        base = 0
        for i in range(t):
            base = base + mine[ORDERS[c][i]] * (D >> (i + 1))
        return base

    def landing(t):
        return D - (D >> t)

    def halving_copy(c, t):
        length = D >> (t + 1)
        bit = ORDERS[c][t]
        away = pl.multiple_of(base_of(c, t) + (1 - mine[bit]) * length, BLOCK)
        return pltpu.make_async_remote_copy(
            src_ref=own_ref.at[c, pl.ds(away, length)],
            dst_ref=rs_recv.at[c, pl.ds(landing(t), length)],
            send_sem=rs_send_sem.at[c, t],
            recv_sem=rs_recv_sem.at[c, t],
            device_id=partners[bit],
            device_id_type=MESH,
        )

    halvings = {}
    sib_copies = {}

    def add_rows(c, first, src_ref, src_first, length):
        step = min(length, 128)

        @pl.loop(0, length // step)
        def _(i):
            to = pl.ds(pl.multiple_of(first + i * step, BLOCK), step)
            frm = pl.ds(pl.multiple_of(src_first + i * step, BLOCK), step)
            own_ref[c, to, :] = (
                own_ref[c, to, :].astype(F32) + src_ref[c, frm, :].astype(F32)
            ).astype(BF16)

    def stage(c, t):
        halvings[c, t].wait_recv()
        add_rows(c, base_of(c, t + 1), rs_recv, landing(t), D >> (t + 1))
        if t + 1 < STEPS:
            halvings[c, t + 1] = halving_copy(c, t + 1)
            halvings[c, t + 1].start()

    gn_ref = acck_ref.at[:ROWS]

    def own_grad(n):
        at = pl.ds(n * TILE, TILE)
        gn_ref[:, n * TILE : (n + 1) * TILE] = (
            lax.dot_general(dq_ref[...], w_ref[at, :D], NT, preferred_element_type=F32)
            + lax.dot_general(
                dk_ref[WINDOW:, :], w_ref[at, D : 2 * D], NT, preferred_element_type=F32
            )
            + lax.dot_general(
                dv_ref[WINDOW:, :], w_ref[at, 2 * D :], NT, preferred_element_type=F32
            )
        )

    def grad_rows(j):
        rows = slice(j * QB, (j + 1) * QB)
        xf = x_ref[rows, :].astype(F32)
        inv = lax.rsqrt(jnp.mean(xf * xf, axis=1, keepdims=True) + EPS)
        normal = xf * inv
        scaled = (gn_ref[rows, :] + back_recv[j].astype(F32)) * gain
        grad = (
            cot_ref[rows, :].astype(F32)
            + (scaled - normal * jnp.mean(scaled * normal, axis=1, keepdims=True)) * inv
        )
        gx_ref[rows, :] = grad.astype(BF16)

    for c in range(CHUNKS):
        weight_half(c, 1 - core, sib_send[c])
        sib_copies[c] = sibling_copy(c)
        sib_copies[c].start()
    for c in range(CHUNKS):
        sib_copies[c].wait_recv()
        weight_half(c, core, own_ref.at[c], sib_recv.at[c])
        halvings[c, 0] = halving_copy(c, 0)
        halvings[c, 0].start()
    for n in range(D // TILE):
        own_grad(n)
    for t in range(STEPS):
        for c in range(CHUNKS):
            stage(c, t)
        if t == 1:
            for j in range(2):
                backs[j].wait_recv()
                grad_rows(j)

    for c in range(CHUNKS):
        rows = pl.ds(pl.multiple_of(base_of(c, STEPS), BLOCK), BLOCK)
        gather_ref[0, :, c * HALF : (c + 1) * HALF] = own_ref[c, rows, :]
    copies = []
    for i, other in enumerate(others):
        copy = pltpu.make_async_remote_copy(
            src_ref=gather_ref.at[0],
            dst_ref=gather_ref.at[i + 1],
            send_sem=gather_sem.at[0, i],
            recv_sem=gather_sem.at[1, i],
            device_id=other,
            device_id_type=MESH,
        )
        copy.start()
        copies.append(copy)
    for j in range(2, NQ):
        backs[j].wait_recv()
        grad_rows(j)
    for i in range(4):
        if i:
            copies[i - 1].wait_recv()
        from_zh = zh if i < 2 else 1 - zh
        from_core = core if i % 2 == 0 else 1 - core
        rows = pl.ds(pl.multiple_of(from_zh * BLOCK, BLOCK), BLOCK)
        for c in range(CHUNKS):
            at = pl.ds(pl.multiple_of(c * 2 * HALF + from_core * HALF, HALF), HALF)
            gw_ref[rows, at] = gather_ref[i, :, c * HALF : (c + 1) * HALF].astype(F32) * 0.25

    for copy in (*halos, *backs.values(), *sib_copies.values(), *halvings.values(), *copies):
        copy.wait_send()


def body(inputs, cotangent, gain, w_qkv, w_out, segment_ids):
    offset = lax.axis_index("seq") * ROWS
    padded = jnp.concatenate([jnp.full((WINDOW,), -1, jnp.int32), segment_ids[0]], 0)
    seg = lax.dynamic_slice_in_dim(padded, offset, EXT, 0)
    any_space = pl.BlockSpec(memory_space=pl.ANY)
    vmem = pl.BlockSpec(memory_space=pltpu.VMEM)
    dma = pltpu.SemaphoreType.DMA
    grad_x, grad_w = pl.pallas_call(
        kernel,
        out_shape=(
            jax.ShapeDtypeStruct((ROWS, D), BF16),
            jax.ShapeDtypeStruct((2 * BLOCK, 3 * D), F32),
        ),
        in_specs=[any_space, any_space, vmem, any_space, any_space, vmem, vmem],
        out_specs=(vmem, vmem),
        scratch_shapes=[
            pltpu.VMEM((ROWS, D), BF16),
            pltpu.VMEM((ROWS, D), BF16),
            pltpu.VMEM((D, 3 * D), BF16),
            pltpu.VMEM((D, D), BF16),
            pltpu.VMEM((WINDOW, D), BF16),
            pltpu.VMEM((EXT, D), BF16),
            pltpu.VMEM((D, EXT), BF16),
            pltpu.VMEM((ROWS, D), BF16),
            pltpu.VMEM((EXT, D), BF16),
            pltpu.VMEM((EXT, D), BF16),
            pltpu.VMEM((D, EXT), BF16),
            pltpu.VMEM((ROWS, D), BF16),
            pltpu.VMEM((NQ, SPAN, QB), F32),
            pltpu.VMEM((ROWS, D), BF16),
            pltpu.VMEM((EXT, D), BF16),
            pltpu.VMEM((EXT, D), BF16),
            pltpu.VMEM((EXT, D), F32),
            pltpu.VMEM((EXT, D), F32),
            pltpu.VMEM((SPAN, 2 * QB), F32),
            pltpu.VMEM((SPAN, 2 * QB), F32),
            pltpu.VMEM((SPAN, 2 * QB), BF16),
            pltpu.VMEM((SPAN, 2 * QB), BF16),
            pltpu.VMEM((SPAN, 2 * QB), BF16),
            pltpu.VMEM((SPAN, 2 * QB), BF16),
            pltpu.VMEM((NQ, QB, D), BF16),
            pltpu.VMEM((NQ, QB, D), BF16),
            pltpu.VMEM((CHUNKS, D, HALF), BF16),
            pltpu.VMEM((CHUNKS, D, HALF), BF16),
            pltpu.VMEM((CHUNKS, D, HALF), BF16),
            pltpu.VMEM((4, BLOCK, CHUNKS * HALF), BF16),
            dma((4,)),
            dma((2, NQ)),
            dma((2, NQ)),
            dma((2, CHUNKS)),
            dma((CHUNKS, STEPS)),
            dma((CHUNKS, STEPS)),
            dma((2, 3)),
        ],
        compiler_params=pltpu.CompilerParams(
            collective_id=0, has_side_effects=True, vmem_limit_bytes=60 * 1024 * 1024
        ),
    )(
        inputs[0],
        cotangent[0],
        gain[None],
        w_qkv,
        w_out,
        seg[None, WINDOW:],
        seg[:, None],
    )
    return grad_x[None], grad_w


def solution(mesh):
    return jax.shard_map(
        body,
        mesh=mesh,
        in_specs=(P("dp", "seq", None), P("dp", "seq", None), P(), P(), P(), P("dp", None)),
        out_specs=(P("dp", "seq", None), P("seq", None)),
        check_vma=False,
    )
```

```python
import functools
import math

import jax
import jax.numpy as jnp
from jax import lax
from jax.experimental import pallas as pl
from jax.experimental.pallas import tpu as pltpu
from jax.sharding import PartitionSpec as P

MESH = pl.DeviceIdType.MESH
F32 = jnp.float32
BF16 = jnp.bfloat16

WINDOW = 512
ROWS = 512
EXT = WINDOW + ROWS
D = 1024
PAIR = 128
PAIRS = D // PAIR
QB = 128
NQ = ROWS // QB
SPAN = WINDOW + QB
TILE = 256
HALF = 256
CHUNKS = 6
EPS = 1e-05
SCALE = 0.125
LOG2E = math.log2(math.e)

NT = (((1,), (1,)), ((), ()))

ORDERS = (
    ("yw", "zu", "yu", "zw", "xw", "xu"),
    ("zw", "yu", "zu", "yw", "xu", "xw"),
    ("yu", "zw", "yw", "zu", "xw", "xu"),
    ("zu", "yw", "zw", "yu", "xu", "xw"),
    ("yw", "zw", "yu", "zu", "xw", "xu"),
    ("zu", "yu", "zw", "yw", "xu", "xw"),
)
STEPS = len(ORDERS[0])
SEQUENCE = (3, 2, 0, 1)
RETURNS = {0: (0, 1), 1: (1, 3)}
BLOCK = 16
BLOCKS = D // BLOCK


def gray(place):
    return {"u": place // 2, "w": (place // 2 + place) % 2}


def block_places(order):
    places = []
    for block in range(BLOCKS):
        zh, seq = block % 2, block // 2
        at = {"x": seq % 4, "y": seq // 4 % 4, "z": zh * 2 + seq // 16}
        place = 0
        for bit in order:
            place = place * 2 + gray(at[bit[0]])[bit[1]]
        places.append(place)
    return places


def kernel(
    x_hbm,
    cot_hbm,
    gain_ref,
    w_hbm,
    wo_hbm,
    segq_ref,
    segk_ref,
    gx_ref,
    gw_ref,
    x_ref,
    cot_ref,
    w_ref,
    wo_ref,
    xh_ref,
    normed_ref,
    nt_ref,
    q_ref,
    k_ref,
    v_ref,
    kt_ref,
    do_ref,
    mask_ref,
    dq_ref,
    dk_ref,
    dv_ref,
    acck_ref,
    accv_ref,
    expo_ref,
    dprob_ref,
    probs_a,
    dscore_a,
    probs_b,
    dscore_b,
    back_send,
    back_recv,
    own_ref,
    sib_recv,
    rs_recv,
    gather_ref,
    load_sem,
    halo_sem,
    back_sem,
    sib_sem,
    rs_send_sem,
    rs_recv_sem,
    gather_sem,
):
    s = lax.axis_index("seq")
    d = lax.axis_index("dp")
    x, y, zl = s % 4, s // 4 % 4, s // 16
    core, zh = d % 2, d // 2
    z = zh * 2 + zl

    def device(x, y, z, core):
        return {"seq": z % 2 * 16 + y * 4 + x, "dp": z // 2 * 2 + core}

    nxt = {"seq": (s + 1) % 32, "dp": d}
    prev = {"seq": (s + 31) % 32, "dp": d}

    def flip(place, bit):
        return 3 - place if bit == "u" else place + 1 - 2 * (place % 2)

    partners = {}
    mine = {}
    for axis, place in (("x", x), ("y", y), ("z", z)):
        for bit in "uw":
            at = {"x": x, "y": y, "z": z, axis: flip(place, bit)}
            partners[axis + bit] = device(at["x"], at["y"], at["z"], core)
            mine[axis + bit] = gray(place)[bit]
    sibling = {"seq": s, "dp": zh * 2 + 1 - core}
    others = [
        {"seq": s, "dp": zh * 2 + 1 - core},
        {"seq": s, "dp": (1 - zh) * 2 + core},
        {"seq": s, "dp": (1 - zh) * 2 + 1 - core},
    ]

    loads = []
    for index, (src, dst) in enumerate(
        ((x_hbm, x_ref), (cot_hbm, cot_ref), (wo_hbm, wo_ref), (w_hbm, w_ref))
    ):
        loads.append(pltpu.make_async_copy(src, dst, load_sem.at[index]))
        loads[-1].start()

    barrier = pltpu.get_barrier_semaphore()
    peers = [nxt, prev, *partners.values(), *others]
    for peer in peers:
        pl.semaphore_signal(barrier, inc=1, device_id=peer, device_id_type=MESH)
    pl.semaphore_wait(barrier, len(peers))

    halos = []
    for piece in range(NQ):
        rows = pl.ds(piece * QB, QB)
        halos.append(
            pltpu.make_async_remote_copy(
                src_ref=x_hbm.at[rows],
                dst_ref=xh_ref.at[rows],
                send_sem=halo_sem.at[0, piece],
                recv_sem=halo_sem.at[1, piece],
                device_id=nxt,
                device_id_type=MESH,
            )
        )
    for piece in reversed(range(NQ)):
        halos[piece].start()

    gain = gain_ref[...]

    def norm_rows(src_ref, row, ext_row):
        xf = src_ref[pl.ds(row, QB), :].astype(F32)
        inv = lax.rsqrt(jnp.mean(xf * xf, axis=1, keepdims=True) + EPS)
        normed = (xf * inv * gain).astype(BF16)
        normed_ref[pl.ds(ext_row, QB), :] = normed
        return normed

    loads[0].wait()

    for j in range(NQ):
        normed = norm_rows(x_ref, j * QB, WINDOW + j * QB)
        nt_ref[:, WINDOW + j * QB : WINDOW + (j + 1) * QB] = normed.T

    lane = lax.broadcasted_iota(jnp.int32, (SPAN, QB), 1)
    row = lax.broadcasted_iota(jnp.int32, (SPAN, QB), 0)
    in_window = (row > lane) & (row <= lane + WINDOW)
    for j in range(NQ):
        same = segk_ref[j * QB : j * QB + SPAN, :] == segq_ref[:, j * QB : (j + 1) * QB]
        mask_ref[j] = jnp.where(in_window & same, 0.0, -1e30).astype(F32)

    loads[1].wait()
    loads[2].wait()

    @pl.loop(0, D // TILE)
    def _(n):
        at = pl.ds(pl.multiple_of(n * TILE, TILE), TILE)
        do_ref[:, at] = lax.dot_general(
            cot_ref[...], wo_ref[at, :], NT, preferred_element_type=F32
        ).astype(BF16)

    loads[3].wait()

    def keys_values(first, count):
        @pl.loop(0, D // TILE)
        def _(n):
            at = pl.ds(pl.multiple_of(n * TILE, TILE), TILE)
            at_k = pl.ds(pl.multiple_of(D + n * TILE, TILE), TILE)
            at_v = pl.ds(pl.multiple_of(2 * D + n * TILE, TILE), TILE)
            normed = normed_ref[first : first + count, :]
            k = jnp.dot(normed, w_ref[:, at_k], preferred_element_type=F32).astype(BF16)
            k_ref[first : first + count, at] = k
            kt_ref[at, first : first + count] = k.T
            v = jnp.dot(normed, w_ref[:, at_v], preferred_element_type=F32).astype(BF16)
            v_ref[first : first + count, at] = v

    @pl.loop(0, D // TILE)
    def _(n):
        at = pl.ds(pl.multiple_of(n * TILE, TILE), TILE)
        q_ref[:, at] = jnp.dot(
            normed_ref[WINDOW:, :], w_ref[:, at], preferred_element_type=F32
        ).astype(BF16)

    keys_values(WINDOW, ROWS)

    first_head = lax.broadcasted_iota(jnp.int32, (QB, PAIR), 1) < PAIR // 2
    zero = jnp.zeros((QB, PAIR), BF16)

    def two_heads(block):
        return jnp.concatenate(
            [jnp.where(first_head, block, zero), jnp.where(first_head, zero, block)], 0
        )

    def scores_of(j, pair, held):
        at = pl.ds(pl.multiple_of(pair * PAIR, PAIR), PAIR)
        span = slice(j * QB, j * QB + SPAN)
        probs_ref, dscore_ref = held
        state = {}

        def scores():
            queries = two_heads(q_ref[j * QB : (j + 1) * QB, at])
            value = lax.dot_general(k_ref[span, at], queries, NT, preferred_element_type=F32)
            mask = mask_ref[j]
            value = value * (SCALE * LOG2E) + jnp.concatenate([mask, mask], 1)
            expo_ref[...] = value
            state["top"] = jnp.max(value, axis=0, keepdims=True)

        def sums():
            grads = two_heads(do_ref[j * QB : (j + 1) * QB, at])
            expo = jnp.exp2(expo_ref[...] - state["top"])
            dprob = lax.dot_general(v_ref[span, at], grads, NT, preferred_element_type=F32)
            expo_ref[...] = expo
            dprob_ref[...] = dprob
            state["inverse"] = 1.0 / jnp.sum(expo, axis=0, keepdims=True)
            total = jnp.sum(expo * dprob, axis=0, keepdims=True)
            state["delta"] = total * state["inverse"]

        def products():
            probs = expo_ref[...] * state["inverse"]
            probs_ref[...] = probs.astype(BF16)
            dscore_ref[...] = (probs * (dprob_ref[...] - state["delta"])).astype(BF16)

        return [scores, sums, products]

    def grads_of(j, pair, held):
        at = pl.ds(pl.multiple_of(pair * PAIR, PAIR), PAIR)
        lo = j * QB
        probs_ref, dscore_ref = held

        def add_up(part, acc_ref, out_ref, scale):
            for r in range(0, SPAN, QB):
                block = (lo + r) // QB
                reached = [i for i in SEQUENCE if i <= block <= i + SPAN // QB - 1]
                rows = slice(lo + r, lo + r + QB)
                value = part[r : r + QB]
                if j != reached[0]:
                    value = acc_ref[rows, at] + value
                if j == reached[-1]:
                    out_ref[rows, at] = (value * scale).astype(BF16)
                else:
                    acc_ref[rows, at] = value

        def values():
            grads = two_heads(do_ref[lo : lo + QB, at])
            part = jnp.dot(probs_ref[...], grads, preferred_element_type=F32)
            add_up(part, accv_ref, dv_ref, 1.0)

        def keys():
            queries = two_heads(q_ref[lo : lo + QB, at])
            part = jnp.dot(dscore_ref[...], queries, preferred_element_type=F32)
            add_up(part, acck_ref, dk_ref, SCALE)

        def queries():
            part = jnp.dot(
                kt_ref[at, lo : lo + SPAN], dscore_ref[...], preferred_element_type=F32
            )
            part = jnp.concatenate([part[: PAIR // 2, :QB], part[PAIR // 2 :, QB:]], 0)
            dq_ref[lo : lo + QB, at] = (part.T * SCALE).astype(BF16)

        return [values, keys, queries]

    def side_by_side(one, other):
        for i in range(3):
            for steps in (one, other):
                if steps:
                    steps[i]()

    def arrive(j):
        halos[j].wait_recv()
        normed = norm_rows(xh_ref, j * QB, j * QB)
        nt_ref[:, j * QB : (j + 1) * QB] = normed.T
        keys_values(j * QB, QB)

    backs = {}

    def give_back(first, count):
        rows = slice(first * QB, (first + count) * QB)

        @pl.loop(0, D // TILE)
        def _(n):
            at = pl.ds(pl.multiple_of(n * TILE, TILE), TILE)
            value = (
                lax.dot_general(
                    dk_ref[rows, :], w_ref[at, D : 2 * D], NT, preferred_element_type=F32
                )
                + lax.dot_general(
                    dv_ref[rows, :], w_ref[at, 2 * D :], NT, preferred_element_type=F32
                )
            ).astype(BF16)
            for i in range(count):
                back_send[first + i, :, at] = value[i * QB : (i + 1) * QB]

        for b in range(first, first + count):
            backs[b] = pltpu.make_async_remote_copy(
                src_ref=back_send.at[b],
                dst_ref=back_recv.at[b],
                send_sem=back_sem.at[0, b],
                recv_sem=back_sem.at[1, b],
                device_id=prev,
                device_id_type=MESH,
            )
            backs[b].start()

    even, odd = (probs_a, dscore_a), (probs_b, dscore_b)
    last = None
    arrived = set()
    for j in SEQUENCE:
        for piece in reversed(range(j, NQ)):
            if piece not in arrived:
                arrived.add(piece)
                arrive(piece)
        side_by_side(scores_of(j, 0, even), last and grads_of(*last))
        if last and last[0] in RETURNS:
            give_back(*RETURNS[last[0]])
        side_by_side(scores_of(j, 1, odd), grads_of(j, 0, even))

        @pl.loop(1, PAIRS // 2)
        def _(p):
            side_by_side(scores_of(j, p * 2, even), grads_of(j, p * 2 - 1, odd))
            side_by_side(scores_of(j, p * 2 + 1, odd), grads_of(j, p * 2, even))

        last = (j, PAIRS - 1, odd)
    side_by_side(None, grads_of(*last))
    give_back(*RETURNS[last[0]])

    places = [block_places(order) for order in ORDERS]
    sib_send = [
        ref.at[:, i * HALF : (i + 1) * HALF] for ref in (k_ref, v_ref) for i in range(D // HALF)
    ]

    def weight_half(c, half, out_ref, add_ref=None):
        part, lo = c // 2, c % 2 * 2 * HALF
        at = pl.ds(pl.multiple_of(lo + half * HALF, HALF), HALF)
        if part == 0:
            value = jnp.dot(
                nt_ref[:, WINDOW:], dq_ref[:, at], preferred_element_type=F32
            )
        else:
            grads = dk_ref if part == 1 else dv_ref
            value = jnp.dot(nt_ref[...], grads[:, at], preferred_element_type=F32)
        for block, place in enumerate(places[c]):
            rows = slice(place * BLOCK, (place + 1) * BLOCK)
            piece = value[block * BLOCK : (block + 1) * BLOCK]
            if add_ref is not None:
                piece = piece + add_ref[rows, :].astype(F32)
            out_ref[rows, :] = piece.astype(BF16)

    def sibling_copy(c):
        return pltpu.make_async_remote_copy(
            src_ref=sib_send[c],
            dst_ref=sib_recv.at[c],
            send_sem=sib_sem.at[0, c],
            recv_sem=sib_sem.at[1, c],
            device_id=sibling,
            device_id_type=MESH,
        )

    def base_of(c, t):
        base = 0
        for i in range(t):
            base = base + mine[ORDERS[c][i]] * (D >> (i + 1))
        return base

    def landing(t):
        return D - (D >> t)

    def halving_copy(c, t):
        length = D >> (t + 1)
        bit = ORDERS[c][t]
        away = pl.multiple_of(base_of(c, t) + (1 - mine[bit]) * length, BLOCK)
        return pltpu.make_async_remote_copy(
            src_ref=own_ref.at[c, pl.ds(away, length)],
            dst_ref=rs_recv.at[c, pl.ds(landing(t), length)],
            send_sem=rs_send_sem.at[c, t],
            recv_sem=rs_recv_sem.at[c, t],
            device_id=partners[bit],
            device_id_type=MESH,
        )

    halvings = {}
    sib_copies = {}

    def add_rows(c, first, src_ref, src_first, length):
        step = min(length, 128)

        @pl.loop(0, length // step)
        def _(i):
            to = pl.ds(pl.multiple_of(first + i * step, BLOCK), step)
            frm = pl.ds(pl.multiple_of(src_first + i * step, BLOCK), step)
            own_ref[c, to, :] = (
                own_ref[c, to, :].astype(F32) + src_ref[c, frm, :].astype(F32)
            ).astype(BF16)

    def stage(c, t):
        halvings[c, t].wait_recv()
        add_rows(c, base_of(c, t + 1), rs_recv, landing(t), D >> (t + 1))
        if t + 1 < STEPS:
            halvings[c, t + 1] = halving_copy(c, t + 1)
            halvings[c, t + 1].start()

    gn_ref = acck_ref.at[:ROWS]

    def own_grad(n):
        at = pl.ds(n * TILE, TILE)
        gn_ref[:, n * TILE : (n + 1) * TILE] = (
            lax.dot_general(dq_ref[...], w_ref[at, :D], NT, preferred_element_type=F32)
            + lax.dot_general(
                dk_ref[WINDOW:, :], w_ref[at, D : 2 * D], NT, preferred_element_type=F32
            )
            + lax.dot_general(
                dv_ref[WINDOW:, :], w_ref[at, 2 * D :], NT, preferred_element_type=F32
            )
        )

    def grad_rows(j):
        rows = slice(j * QB, (j + 1) * QB)
        xf = x_ref[rows, :].astype(F32)
        inv = lax.rsqrt(jnp.mean(xf * xf, axis=1, keepdims=True) + EPS)
        normal = xf * inv
        scaled = (gn_ref[rows, :] + back_recv[j].astype(F32)) * gain
        grad = (
            cot_ref[rows, :].astype(F32)
            + (scaled - normal * jnp.mean(scaled * normal, axis=1, keepdims=True)) * inv
        )
        gx_ref[rows, :] = grad.astype(BF16)

    for c in range(CHUNKS):
        weight_half(c, 1 - core, sib_send[c])
        sib_copies[c] = sibling_copy(c)
        sib_copies[c].start()
    for c in range(CHUNKS):
        sib_copies[c].wait_recv()
        weight_half(c, core, own_ref.at[c], sib_recv.at[c])
        halvings[c, 0] = halving_copy(c, 0)
        halvings[c, 0].start()
    for n in range(D // TILE):
        own_grad(n)
    for t in range(STEPS):
        for c in range(CHUNKS):
            stage(c, t)
        if t == 1:
            for j in range(2):
                backs[j].wait_recv()
                grad_rows(j)

    for c in range(CHUNKS):
        rows = pl.ds(pl.multiple_of(base_of(c, STEPS), BLOCK), BLOCK)
        gather_ref[0, :, c * HALF : (c + 1) * HALF] = own_ref[c, rows, :]
    copies = []
    for i, other in enumerate(others):
        copy = pltpu.make_async_remote_copy(
            src_ref=gather_ref.at[0],
            dst_ref=gather_ref.at[i + 1],
            send_sem=gather_sem.at[0, i],
            recv_sem=gather_sem.at[1, i],
            device_id=other,
            device_id_type=MESH,
        )
        copy.start()
        copies.append(copy)
    for j in range(2, NQ):
        backs[j].wait_recv()
        grad_rows(j)
    for i in range(4):
        if i:
            copies[i - 1].wait_recv()
        from_zh = zh if i < 2 else 1 - zh
        from_core = core if i % 2 == 0 else 1 - core
        rows = pl.ds(pl.multiple_of(from_zh * BLOCK, BLOCK), BLOCK)
        for c in range(CHUNKS):
            at = pl.ds(pl.multiple_of(c * 2 * HALF + from_core * HALF, HALF), HALF)
            gw_ref[rows, at] = gather_ref[i, :, c * HALF : (c + 1) * HALF]

    for copy in (*halos, *backs.values(), *sib_copies.values(), *halvings.values(), *copies):
        copy.wait_send()


def body(inputs, cotangent, gain, w_qkv, w_out, segment_ids):
    offset = lax.axis_index("seq") * ROWS
    padded = jnp.concatenate([jnp.full((WINDOW,), -1, jnp.int32), segment_ids[0]], 0)
    seg = lax.dynamic_slice_in_dim(padded, offset, EXT, 0)
    any_space = pl.BlockSpec(memory_space=pl.ANY)
    vmem = pl.BlockSpec(memory_space=pltpu.VMEM)
    dma = pltpu.SemaphoreType.DMA
    grad_x, grad_w = pl.pallas_call(
        kernel,
        out_shape=(
            jax.ShapeDtypeStruct((ROWS, D), BF16),
            jax.ShapeDtypeStruct((2 * BLOCK, 3 * D), BF16),
        ),
        in_specs=[any_space, any_space, vmem, any_space, any_space, vmem, vmem],
        out_specs=(vmem, vmem),
        scratch_shapes=[
            pltpu.VMEM((ROWS, D), BF16),
            pltpu.VMEM((ROWS, D), BF16),
            pltpu.VMEM((D, 3 * D), BF16),
            pltpu.VMEM((D, D), BF16),
            pltpu.VMEM((WINDOW, D), BF16),
            pltpu.VMEM((EXT, D), BF16),
            pltpu.VMEM((D, EXT), BF16),
            pltpu.VMEM((ROWS, D), BF16),
            pltpu.VMEM((EXT, D), BF16),
            pltpu.VMEM((EXT, D), BF16),
            pltpu.VMEM((D, EXT), BF16),
            pltpu.VMEM((ROWS, D), BF16),
            pltpu.VMEM((NQ, SPAN, QB), F32),
            pltpu.VMEM((ROWS, D), BF16),
            pltpu.VMEM((EXT, D), BF16),
            pltpu.VMEM((EXT, D), BF16),
            pltpu.VMEM((EXT, D), F32),
            pltpu.VMEM((EXT, D), F32),
            pltpu.VMEM((SPAN, 2 * QB), F32),
            pltpu.VMEM((SPAN, 2 * QB), F32),
            pltpu.VMEM((SPAN, 2 * QB), BF16),
            pltpu.VMEM((SPAN, 2 * QB), BF16),
            pltpu.VMEM((SPAN, 2 * QB), BF16),
            pltpu.VMEM((SPAN, 2 * QB), BF16),
            pltpu.VMEM((NQ, QB, D), BF16),
            pltpu.VMEM((NQ, QB, D), BF16),
            pltpu.VMEM((CHUNKS, D, HALF), BF16),
            pltpu.VMEM((CHUNKS, D, HALF), BF16),
            pltpu.VMEM((CHUNKS, D, HALF), BF16),
            pltpu.VMEM((4, BLOCK, CHUNKS * HALF), BF16),
            dma((4,)),
            dma((2, NQ)),
            dma((2, NQ)),
            dma((2, CHUNKS)),
            dma((CHUNKS, STEPS)),
            dma((CHUNKS, STEPS)),
            dma((2, 3)),
        ],
        compiler_params=pltpu.CompilerParams(
            collective_id=0, has_side_effects=True, vmem_limit_bytes=60 * 1024 * 1024
        ),
    )(
        inputs[0],
        cotangent[0],
        gain[None],
        w_qkv,
        w_out,
        seg[None, WINDOW:],
        seg[:, None],
    )
    return grad_x[None], grad_w.astype(F32) * (1 / 4)


def solution(mesh):
    return jax.shard_map(
        body,
        mesh=mesh,
        in_specs=(P("dp", "seq", None), P("dp", "seq", None), P(), P(), P(), P("dp", None)),
        out_specs=(P("dp", "seq", None), P("seq", None)),
        check_vma=False,
    )
```

```python
import functools
import math

import jax
import jax.numpy as jnp
from jax import lax
from jax.experimental import pallas as pl
from jax.experimental.pallas import tpu as pltpu
from jax.sharding import PartitionSpec as P

MESH = pl.DeviceIdType.MESH
F32 = jnp.float32
BF16 = jnp.bfloat16

WINDOW = 512
ROWS = 512
EXT = WINDOW + ROWS
D = 1024
PAIR = 128
PAIRS = D // PAIR
QB = 128
NQ = ROWS // QB
SPAN = WINDOW + QB
TILE = 256
HALF = 256
CHUNKS = 6
EPS = 1e-05
SCALE = 0.125
LOG2E = math.log2(math.e)

NT = (((1,), (1,)), ((), ()))

ORDERS = (
    ("yw", "zu", "yu", "zw", "xw", "xu"),
    ("zw", "yu", "zu", "yw", "xu", "xw"),
    ("yu", "zw", "yw", "zu", "xw", "xu"),
    ("zu", "yw", "zw", "yu", "xu", "xw"),
    ("yw", "zw", "yu", "zu", "xw", "xu"),
    ("zu", "yu", "zw", "yw", "xu", "xw"),
)
STEPS = len(ORDERS[0])
SEQUENCE = (3, 2, 0, 1)
RETURNS = {0: (0, 1), 1: (1, 3)}
BLOCK = 16
BLOCKS = D // BLOCK


def gray(place):
    return {"u": place // 2, "w": (place // 2 + place) % 2}


def block_places(order):
    places = []
    for block in range(BLOCKS):
        zh, seq = block % 2, block // 2
        at = {"x": seq % 4, "y": seq // 4 % 4, "z": zh * 2 + seq // 16}
        place = 0
        for bit in order:
            place = place * 2 + gray(at[bit[0]])[bit[1]]
        places.append(place)
    return places


def kernel(
    x_hbm,
    cot_hbm,
    gain_ref,
    w_hbm,
    wo_hbm,
    seg_ref,
    gx_ref,
    gw_ref,
    x_ref,
    cot_ref,
    w_ref,
    wo_ref,
    xh_ref,
    normed_ref,
    nt_ref,
    q_ref,
    k_ref,
    v_ref,
    kt_ref,
    do_ref,
    mask_ref,
    dq_ref,
    dk_ref,
    dv_ref,
    acck_ref,
    accv_ref,
    expo_ref,
    dprob_ref,
    probs_a,
    dscore_a,
    probs_b,
    dscore_b,
    back_send,
    back_recv,
    own_ref,
    sib_recv,
    rs_recv,
    gather_ref,
    load_sem,
    halo_sem,
    back_sem,
    sib_sem,
    rs_send_sem,
    rs_recv_sem,
    gather_sem,
):
    s = lax.axis_index("seq")
    d = lax.axis_index("dp")
    x, y, zl = s % 4, s // 4 % 4, s // 16
    core, zh = d % 2, d // 2
    z = zh * 2 + zl

    def device(x, y, z, core):
        return {"seq": z % 2 * 16 + y * 4 + x, "dp": z // 2 * 2 + core}

    nxt = {"seq": (s + 1) % 32, "dp": d}
    prev = {"seq": (s + 31) % 32, "dp": d}

    def flip(place, bit):
        return 3 - place if bit == "u" else place + 1 - 2 * (place % 2)

    partners = {}
    mine = {}
    for axis, place in (("x", x), ("y", y), ("z", z)):
        for bit in "uw":
            at = {"x": x, "y": y, "z": z, axis: flip(place, bit)}
            partners[axis + bit] = device(at["x"], at["y"], at["z"], core)
            mine[axis + bit] = gray(place)[bit]
    sibling = {"seq": s, "dp": zh * 2 + 1 - core}
    others = [
        {"seq": s, "dp": zh * 2 + 1 - core},
        {"seq": s, "dp": (1 - zh) * 2 + core},
        {"seq": s, "dp": (1 - zh) * 2 + 1 - core},
    ]

    loads = []
    for index, (src, dst) in enumerate(
        ((x_hbm, x_ref), (cot_hbm, cot_ref), (wo_hbm, wo_ref), (w_hbm, w_ref))
    ):
        loads.append(pltpu.make_async_copy(src, dst, load_sem.at[index]))
        loads[-1].start()

    barrier = pltpu.get_barrier_semaphore()
    peers = [nxt, prev, *partners.values(), *others]
    for peer in peers:
        pl.semaphore_signal(barrier, inc=1, device_id=peer, device_id_type=MESH)
    pl.semaphore_wait(barrier, len(peers))

    halos = []
    for piece in range(NQ):
        rows = pl.ds(piece * QB, QB)
        halos.append(
            pltpu.make_async_remote_copy(
                src_ref=x_hbm.at[rows],
                dst_ref=xh_ref.at[rows],
                send_sem=halo_sem.at[0, piece],
                recv_sem=halo_sem.at[1, piece],
                device_id=nxt,
                device_id_type=MESH,
            )
        )
    for piece in reversed(range(NQ)):
        halos[piece].start()

    gain = gain_ref[...]

    def norm_rows(src_ref, row, ext_row):
        xf = src_ref[pl.ds(row, QB), :].astype(F32)
        inv = lax.rsqrt(jnp.mean(xf * xf, axis=1, keepdims=True) + EPS)
        normed = (xf * inv * gain).astype(BF16)
        normed_ref[pl.ds(ext_row, QB), :] = normed
        return normed

    loads[0].wait()

    for j in range(NQ):
        normed = norm_rows(x_ref, j * QB, WINDOW + j * QB)
        nt_ref[:, WINDOW + j * QB : WINDOW + (j + 1) * QB] = normed.T

    lane = lax.broadcasted_iota(jnp.int32, (SPAN, QB), 1)
    row = lax.broadcasted_iota(jnp.int32, (SPAN, QB), 0)
    in_window = (row > lane) & (row <= lane + WINDOW)
    seg = seg_ref[...].astype(F32)
    seg_keys = jnp.broadcast_to(seg, (QB, EXT)).T
    for j in range(NQ):
        seg_queries = seg[:, WINDOW + j * QB : WINDOW + (j + 1) * QB]
        same = seg_keys[j * QB : j * QB + SPAN, :] == seg_queries
        mask_ref[j] = jnp.where(in_window & same, 0.0, -1e30).astype(F32)

    loads[1].wait()
    loads[2].wait()

    @pl.loop(0, D // TILE)
    def _(n):
        at = pl.ds(pl.multiple_of(n * TILE, TILE), TILE)
        do_ref[:, at] = lax.dot_general(
            cot_ref[...], wo_ref[at, :], NT, preferred_element_type=F32
        ).astype(BF16)

    loads[3].wait()

    def keys_values(first, count):
        @pl.loop(0, D // TILE)
        def _(n):
            at = pl.ds(pl.multiple_of(n * TILE, TILE), TILE)
            at_k = pl.ds(pl.multiple_of(D + n * TILE, TILE), TILE)
            at_v = pl.ds(pl.multiple_of(2 * D + n * TILE, TILE), TILE)
            normed = normed_ref[first : first + count, :]
            k = jnp.dot(normed, w_ref[:, at_k], preferred_element_type=F32).astype(BF16)
            k_ref[first : first + count, at] = k
            kt_ref[at, first : first + count] = k.T
            v = jnp.dot(normed, w_ref[:, at_v], preferred_element_type=F32).astype(BF16)
            v_ref[first : first + count, at] = v

    @pl.loop(0, D // TILE)
    def _(n):
        at = pl.ds(pl.multiple_of(n * TILE, TILE), TILE)
        q_ref[:, at] = jnp.dot(
            normed_ref[WINDOW:, :], w_ref[:, at], preferred_element_type=F32
        ).astype(BF16)

    keys_values(WINDOW, ROWS)

    first_head = lax.broadcasted_iota(jnp.int32, (QB, PAIR), 1) < PAIR // 2
    zero = jnp.zeros((QB, PAIR), BF16)

    def two_heads(block):
        return jnp.concatenate(
            [jnp.where(first_head, block, zero), jnp.where(first_head, zero, block)], 0
        )

    def scores_of(j, pair, held):
        at = pl.ds(pl.multiple_of(pair * PAIR, PAIR), PAIR)
        span = slice(j * QB, j * QB + SPAN)
        probs_ref, dscore_ref = held
        state = {}

        def scores():
            queries = two_heads(q_ref[j * QB : (j + 1) * QB, at])
            value = lax.dot_general(k_ref[span, at], queries, NT, preferred_element_type=F32)
            mask = mask_ref[j]
            value = value * (SCALE * LOG2E) + jnp.concatenate([mask, mask], 1)
            expo_ref[...] = value
            state["top"] = jnp.max(value, axis=0, keepdims=True)

        def sums():
            grads = two_heads(do_ref[j * QB : (j + 1) * QB, at])
            expo = jnp.exp2(expo_ref[...] - state["top"])
            dprob = lax.dot_general(v_ref[span, at], grads, NT, preferred_element_type=F32)
            expo_ref[...] = expo
            dprob_ref[...] = dprob
            state["inverse"] = 1.0 / jnp.sum(expo, axis=0, keepdims=True)
            total = jnp.sum(expo * dprob, axis=0, keepdims=True)
            state["delta"] = total * state["inverse"]

        def products():
            probs = expo_ref[...] * state["inverse"]
            probs_ref[...] = probs.astype(BF16)
            dscore_ref[...] = (probs * (dprob_ref[...] - state["delta"])).astype(BF16)

        return [scores, sums, products]

    def grads_of(j, pair, held):
        at = pl.ds(pl.multiple_of(pair * PAIR, PAIR), PAIR)
        lo = j * QB
        probs_ref, dscore_ref = held

        def add_up(part, acc_ref, out_ref, scale):
            for r in range(0, SPAN, QB):
                block = (lo + r) // QB
                reached = [i for i in SEQUENCE if i <= block <= i + SPAN // QB - 1]
                rows = slice(lo + r, lo + r + QB)
                value = part[r : r + QB]
                if j != reached[0]:
                    value = acc_ref[rows, at] + value
                if j == reached[-1]:
                    out_ref[rows, at] = (value * scale).astype(BF16)
                else:
                    acc_ref[rows, at] = value

        def values():
            grads = two_heads(do_ref[lo : lo + QB, at])
            part = jnp.dot(probs_ref[...], grads, preferred_element_type=F32)
            add_up(part, accv_ref, dv_ref, 1.0)

        def keys():
            queries = two_heads(q_ref[lo : lo + QB, at])
            part = jnp.dot(dscore_ref[...], queries, preferred_element_type=F32)
            add_up(part, acck_ref, dk_ref, SCALE)

        def queries():
            part = jnp.dot(
                kt_ref[at, lo : lo + SPAN], dscore_ref[...], preferred_element_type=F32
            )
            part = jnp.concatenate([part[: PAIR // 2, :QB], part[PAIR // 2 :, QB:]], 0)
            dq_ref[lo : lo + QB, at] = (part.T * SCALE).astype(BF16)

        return [values, keys, queries]

    def side_by_side(one, other):
        for i in range(3):
            for steps in (one, other):
                if steps:
                    steps[i]()

    def arrive(j):
        halos[j].wait_recv()
        normed = norm_rows(xh_ref, j * QB, j * QB)
        nt_ref[:, j * QB : (j + 1) * QB] = normed.T
        keys_values(j * QB, QB)

    backs = {}

    def give_back(first, count):
        rows = slice(first * QB, (first + count) * QB)

        @pl.loop(0, D // TILE)
        def _(n):
            at = pl.ds(pl.multiple_of(n * TILE, TILE), TILE)
            value = (
                lax.dot_general(
                    dk_ref[rows, :], w_ref[at, D : 2 * D], NT, preferred_element_type=F32
                )
                + lax.dot_general(
                    dv_ref[rows, :], w_ref[at, 2 * D :], NT, preferred_element_type=F32
                )
            ).astype(BF16)
            for i in range(count):
                back_send[first + i, :, at] = value[i * QB : (i + 1) * QB]

        for b in range(first, first + count):
            backs[b] = pltpu.make_async_remote_copy(
                src_ref=back_send.at[b],
                dst_ref=back_recv.at[b],
                send_sem=back_sem.at[0, b],
                recv_sem=back_sem.at[1, b],
                device_id=prev,
                device_id_type=MESH,
            )
            backs[b].start()

    even, odd = (probs_a, dscore_a), (probs_b, dscore_b)
    last = None
    arrived = set()
    for j in SEQUENCE:
        for piece in reversed(range(j, NQ)):
            if piece not in arrived:
                arrived.add(piece)
                arrive(piece)
        side_by_side(scores_of(j, 0, even), last and grads_of(*last))
        if last and last[0] in RETURNS:
            give_back(*RETURNS[last[0]])
        side_by_side(scores_of(j, 1, odd), grads_of(j, 0, even))

        @pl.loop(1, PAIRS // 2)
        def _(p):
            side_by_side(scores_of(j, p * 2, even), grads_of(j, p * 2 - 1, odd))
            side_by_side(scores_of(j, p * 2 + 1, odd), grads_of(j, p * 2, even))

        last = (j, PAIRS - 1, odd)
    side_by_side(None, grads_of(*last))
    give_back(*RETURNS[last[0]])

    places = [block_places(order) for order in ORDERS]
    sib_send = [
        ref.at[:, i * HALF : (i + 1) * HALF] for ref in (k_ref, v_ref) for i in range(D // HALF)
    ]

    def weight_half(c, half, out_ref, add_ref=None):
        part, lo = c // 2, c % 2 * 2 * HALF
        at = pl.ds(pl.multiple_of(lo + half * HALF, HALF), HALF)
        if part == 0:
            value = jnp.dot(
                nt_ref[:, WINDOW:], dq_ref[:, at], preferred_element_type=F32
            )
        else:
            grads = dk_ref if part == 1 else dv_ref
            value = jnp.dot(nt_ref[...], grads[:, at], preferred_element_type=F32)
        for block, place in enumerate(places[c]):
            rows = slice(place * BLOCK, (place + 1) * BLOCK)
            piece = value[block * BLOCK : (block + 1) * BLOCK]
            if add_ref is not None:
                piece = piece + add_ref[rows, :].astype(F32)
            out_ref[rows, :] = piece.astype(BF16)

    def sibling_copy(c):
        return pltpu.make_async_remote_copy(
            src_ref=sib_send[c],
            dst_ref=sib_recv.at[c],
            send_sem=sib_sem.at[0, c],
            recv_sem=sib_sem.at[1, c],
            device_id=sibling,
            device_id_type=MESH,
        )

    def base_of(c, t):
        base = 0
        for i in range(t):
            base = base + mine[ORDERS[c][i]] * (D >> (i + 1))
        return base

    def landing(t):
        return D - (D >> t)

    def halving_copy(c, t):
        length = D >> (t + 1)
        bit = ORDERS[c][t]
        away = pl.multiple_of(base_of(c, t) + (1 - mine[bit]) * length, BLOCK)
        return pltpu.make_async_remote_copy(
            src_ref=own_ref.at[c, pl.ds(away, length)],
            dst_ref=rs_recv.at[c, pl.ds(landing(t), length)],
            send_sem=rs_send_sem.at[c, t],
            recv_sem=rs_recv_sem.at[c, t],
            device_id=partners[bit],
            device_id_type=MESH,
        )

    halvings = {}
    sib_copies = {}

    def add_rows(c, first, src_ref, src_first, length):
        step = min(length, 128)

        @pl.loop(0, length // step)
        def _(i):
            to = pl.ds(pl.multiple_of(first + i * step, BLOCK), step)
            frm = pl.ds(pl.multiple_of(src_first + i * step, BLOCK), step)
            own_ref[c, to, :] = (
                own_ref[c, to, :].astype(F32) + src_ref[c, frm, :].astype(F32)
            ).astype(BF16)

    def stage(c, t):
        halvings[c, t].wait_recv()
        add_rows(c, base_of(c, t + 1), rs_recv, landing(t), D >> (t + 1))
        if t + 1 < STEPS:
            halvings[c, t + 1] = halving_copy(c, t + 1)
            halvings[c, t + 1].start()

    gn_ref = acck_ref.at[:ROWS]

    def own_grad(n):
        at = pl.ds(n * TILE, TILE)
        gn_ref[:, n * TILE : (n + 1) * TILE] = (
            lax.dot_general(dq_ref[...], w_ref[at, :D], NT, preferred_element_type=F32)
            + lax.dot_general(
                dk_ref[WINDOW:, :], w_ref[at, D : 2 * D], NT, preferred_element_type=F32
            )
            + lax.dot_general(
                dv_ref[WINDOW:, :], w_ref[at, 2 * D :], NT, preferred_element_type=F32
            )
        )

    def grad_rows(j):
        rows = slice(j * QB, (j + 1) * QB)
        xf = x_ref[rows, :].astype(F32)
        inv = lax.rsqrt(jnp.mean(xf * xf, axis=1, keepdims=True) + EPS)
        normal = xf * inv
        scaled = (gn_ref[rows, :] + back_recv[j].astype(F32)) * gain
        grad = (
            cot_ref[rows, :].astype(F32)
            + (scaled - normal * jnp.mean(scaled * normal, axis=1, keepdims=True)) * inv
        )
        gx_ref[rows, :] = grad.astype(BF16)

    for c in range(CHUNKS):
        weight_half(c, 1 - core, sib_send[c])
        sib_copies[c] = sibling_copy(c)
        sib_copies[c].start()
    for c in range(CHUNKS):
        sib_copies[c].wait_recv()
        weight_half(c, core, own_ref.at[c], sib_recv.at[c])
        halvings[c, 0] = halving_copy(c, 0)
        halvings[c, 0].start()
    for n in range(D // TILE):
        own_grad(n)
    for t in range(STEPS):
        for c in range(CHUNKS):
            stage(c, t)
        if t == 1:
            for j in range(2):
                backs[j].wait_recv()
                grad_rows(j)

    for c in range(CHUNKS):
        rows = pl.ds(pl.multiple_of(base_of(c, STEPS), BLOCK), BLOCK)
        gather_ref[0, :, c * HALF : (c + 1) * HALF] = own_ref[c, rows, :]
    copies = []
    for i, other in enumerate(others):
        copy = pltpu.make_async_remote_copy(
            src_ref=gather_ref.at[0],
            dst_ref=gather_ref.at[i + 1],
            send_sem=gather_sem.at[0, i],
            recv_sem=gather_sem.at[1, i],
            device_id=other,
            device_id_type=MESH,
        )
        copy.start()
        copies.append(copy)
    for j in range(2, NQ):
        backs[j].wait_recv()
        grad_rows(j)
    for i in range(4):
        if i:
            copies[i - 1].wait_recv()
        from_zh = zh if i < 2 else 1 - zh
        from_core = core if i % 2 == 0 else 1 - core
        rows = pl.ds(pl.multiple_of(from_zh * BLOCK, BLOCK), BLOCK)
        for c in range(CHUNKS):
            at = pl.ds(pl.multiple_of(c * 2 * HALF + from_core * HALF, HALF), HALF)
            gw_ref[rows, at] = gather_ref[i, :, c * HALF : (c + 1) * HALF]

    for copy in (*halos, *backs.values(), *sib_copies.values(), *halvings.values(), *copies):
        copy.wait_send()


def body(inputs, cotangent, gain, w_qkv, w_out, segment_ids):
    offset = lax.axis_index("seq") * ROWS
    padded = jnp.concatenate([jnp.full((WINDOW,), -1, jnp.int32), segment_ids[0]], 0)
    seg = lax.dynamic_slice_in_dim(padded, offset, EXT, 0)
    any_space = pl.BlockSpec(memory_space=pl.ANY)
    vmem = pl.BlockSpec(memory_space=pltpu.VMEM)
    dma = pltpu.SemaphoreType.DMA
    grad_x, grad_w = pl.pallas_call(
        kernel,
        out_shape=(
            jax.ShapeDtypeStruct((ROWS, D), BF16),
            jax.ShapeDtypeStruct((2 * BLOCK, 3 * D), BF16),
        ),
        in_specs=[any_space, any_space, vmem, any_space, any_space, vmem],
        out_specs=(vmem, vmem),
        scratch_shapes=[
            pltpu.VMEM((ROWS, D), BF16),
            pltpu.VMEM((ROWS, D), BF16),
            pltpu.VMEM((D, 3 * D), BF16),
            pltpu.VMEM((D, D), BF16),
            pltpu.VMEM((WINDOW, D), BF16),
            pltpu.VMEM((EXT, D), BF16),
            pltpu.VMEM((D, EXT), BF16),
            pltpu.VMEM((ROWS, D), BF16),
            pltpu.VMEM((EXT, D), BF16),
            pltpu.VMEM((EXT, D), BF16),
            pltpu.VMEM((D, EXT), BF16),
            pltpu.VMEM((ROWS, D), BF16),
            pltpu.VMEM((NQ, SPAN, QB), F32),
            pltpu.VMEM((ROWS, D), BF16),
            pltpu.VMEM((EXT, D), BF16),
            pltpu.VMEM((EXT, D), BF16),
            pltpu.VMEM((EXT, D), F32),
            pltpu.VMEM((EXT, D), F32),
            pltpu.VMEM((SPAN, 2 * QB), F32),
            pltpu.VMEM((SPAN, 2 * QB), F32),
            pltpu.VMEM((SPAN, 2 * QB), BF16),
            pltpu.VMEM((SPAN, 2 * QB), BF16),
            pltpu.VMEM((SPAN, 2 * QB), BF16),
            pltpu.VMEM((SPAN, 2 * QB), BF16),
            pltpu.VMEM((NQ, QB, D), BF16),
            pltpu.VMEM((NQ, QB, D), BF16),
            pltpu.VMEM((CHUNKS, D, HALF), BF16),
            pltpu.VMEM((CHUNKS, D, HALF), BF16),
            pltpu.VMEM((CHUNKS, D, HALF), BF16),
            pltpu.VMEM((4, BLOCK, CHUNKS * HALF), BF16),
            dma((4,)),
            dma((2, NQ)),
            dma((2, NQ)),
            dma((2, CHUNKS)),
            dma((CHUNKS, STEPS)),
            dma((CHUNKS, STEPS)),
            dma((2, 3)),
        ],
        compiler_params=pltpu.CompilerParams(
            collective_id=0, has_side_effects=True, vmem_limit_bytes=60 * 1024 * 1024
        ),
    )(
        inputs[0],
        cotangent[0],
        gain[None],
        w_qkv,
        w_out,
        seg[None],
    )
    return grad_x[None], grad_w.astype(F32) * (1 / 4)


def solution(mesh):
    return jax.shard_map(
        body,
        mesh=mesh,
        in_specs=(P("dp", "seq", None), P("dp", "seq", None), P(), P(), P(), P("dp", None)),
        out_specs=(P("dp", "seq", None), P("seq", None)),
        check_vma=False,
    )
```
